256 devices in a mesh: sec: 2 (over z_lo), band: 32 (over y, x, core), fld: 4 (over z_hi).
Axes of the slice: x: 4, y: 4, z: 8 (z_hi: 4, z_lo: 2; z = z_hi * 2 + z_lo), core: 2. Of those that a mesh axis runs over, the one named last changes fastest.
Arguments:
- grid: bfloat16 [4, 16, 1280, 2688], P('fld', 'sec', 'band'), may hold values from -6 to 6
- legendre: bfloat16 [768, 1280, 768], P(('band', 'fld'), None, 'sec'), may hold values from -0.15625 to 0.15625
- counts: int32 [32], replicated, may hold values from 1 to 1024, 16384 in all
- blocks: int32 [32768], P('band'), may hold values from 0 to 839
- interp: bfloat16 [32768, 128], P('band'), may hold values from -0.5 to 0.5
- source_weights: bfloat16 [64, 2048], replicated, may hold values from -0.75 to 0.75
- inverses: bfloat16 [64, 32, 32], replicated, may hold values from -1 to 1
Outputs:
- spectral: bfloat16 [768, 2, 4, 16, 768], P(('band', 'fld'), None, None, None, 'sec')
- heating: bfloat16 [16, 1280, 2688], P(('sec', 'fld'), 'band')
The draws below stay inside these ranges and needn't reach their ends.
Inputs may be any that keep to these rules, and one draw needn't show every extreme that they name: Band b has counts[b] live slots, slots 0 to counts[b] - 1; the counts sum to 16384 and the largest is 1024.
All inputs are finite; a program needn't handle non-finite values.
Results may differ from the reference program's by a relative error of at most 0.0085.
Values may be sent and summed in bfloat16 or wider, within the bound.
A program may use at most 64 MiB of HBM per device.

```python
import math
import jax
import jax.numpy as jnp
import numpy as np
from jax import lax

FIELDS = 4
LEV = 16
LON = 2688
LAT_DEV = 40
LAT = 1280
M = 768
BANDS = 64
FLUX = 32
CAP = 1024
NBLK = 840
COARSE = 16384
N_BAND = 32


def with_ends(entries, rng, low, high):
    dims = entries.shape
    index_at = [jax.random.randint(jax.random.fold_in(rng, axis), (), 0, dims[axis]) for axis in range(len(dims))]
    entries = entries.at[tuple(index_at)].set(low)
    longest = dims.index(max(dims))
    index_at[longest] = (index_at[longest] + 1) % dims[longest]
    return entries.at[tuple(index_at)].set(high)


def steps_of(stream_key, dims, cuts, smallest, top_value):
    factor_of = 1.0
    for dim, shards_of in cuts:
        heights = jax.random.uniform(jax.random.fold_in(jax.random.fold_in(stream_key, 6), dim), (shards_of,), jnp.float32, smallest / len(cuts), top_value / len(cuts))
        factor_of = factor_of * jnp.repeat(jnp.exp(heights), dims[dim] // shards_of).reshape((-1,) + (1,) * (len(dims) - 1 - dim))
    return factor_of


def split_up(number_of, total, most, slope):
    portions = [(1 << 20) // math.isqrt(standing ** slope) + 1 for standing in range(2, number_of + 1)]
    rest, holding = total - most - (number_of - 1), [1] * (number_of - 1)
    while rest > 0:
        candidates = [i for i in range(number_of - 1) if holding[i] < most]
        mass, remaining = sum([portions[i] for i in candidates]), rest
        for i in candidates:
            addition = min(most - holding[i], max(1, remaining * portions[i] // mass), rest)
            holding[i] = holding[i] + addition
            rest = rest - addition
    return np.array([most] + holding)


def uneven_parts(own_key, count, total, limit, lean):
    if count == 2:
        one = jax.random.randint(own_key, (), max(1, total - limit), min(limit, total - 1) + 1)
        return jnp.stack([one, total - one])
    tallies = jnp.asarray(split_up(count, total, limit, lean), jnp.int32)
    pairs = (count - 1) // 2
    donor, receiver = tallies[1:1 + 2 * pairs:2], tallies[2:2 + 2 * pairs:2]
    margin = jnp.minimum(donor - 1, limit - receiver)
    shifted = jax.random.randint(jax.random.fold_in(own_key, 1), (pairs,), 0, 1 << 20) % (margin + 1)
    tallies = tallies.at[1:1 + 2 * pairs:2].set(donor - shifted).at[2:2 + 2 * pairs:2].set(receiver + shifted)
    return tallies[jax.random.permutation(jax.random.fold_in(own_key, 2), count)]


def scatter_about(stream_key, dims, scale, reach, split=(), kind=jnp.bfloat16):
    array = scale * jax.random.normal(stream_key, dims, jnp.float32)
    if split:
        array = array * steps_of(stream_key, dims, split, -0.22, 0.18)
    return jnp.clip(array, -reach, reach).astype(kind)


def setup_inputs(seed: int = 0) -> dict:
    streams_of = jax.random.split(jax.random.key(seed), 8)
    return {
        "grid": scatter_about(streams_of[0], (FIELDS, LEV, LAT, LON), 1.0, 6.0, ((0, 4), (1, 2), (2, 32))),
        "legendre": scatter_about(streams_of[1], (M, LAT, M), LAT ** -0.5, 0.15625, ((0, 128), (2, 2))),
        "counts": uneven_parts(streams_of[2], N_BAND, COARSE, CAP, 2).astype(jnp.int32),
        "blocks": with_ends(jax.random.randint(streams_of[3], (N_BAND * CAP,), 0, NBLK), jax.random.fold_in(streams_of[3], 1), 0, NBLK - 1).astype(jnp.int32),
        "interp": scatter_about(streams_of[4], (N_BAND * CAP, 128), 128 ** -0.5, 0.5, ((0, 32),)),
        "source_weights": scatter_about(streams_of[5], (FIELDS * LEV, BANDS * FLUX), (FIELDS * LEV) ** -0.5, 0.75),
        "inverses": scatter_about(streams_of[6], (BANDS, FLUX, FLUX), FLUX ** -0.5, 1.0),
    }


def dft_table(lon, waves):
    column = jnp.arange(2 * waves, dtype=jnp.int32)
    wave = column // 2
    part = column % 2
    place = jnp.arange(lon, dtype=jnp.int32)
    phase = place[:, None] * wave[None, :] % lon
    angle = phase.astype(jnp.float32) * (2.0 * math.pi / lon)
    values = jnp.where(part[None, :] == 0, jnp.cos(angle), -jnp.sin(angle))
    return (values * (1.0 / math.sqrt(lon))).astype(jnp.bfloat16)

def heat_rates(flux, count, start):
    levels = flux.shape[0] // 2
    width = flux.shape[1]
    upward = flux[:levels]
    downward = flux[levels:]
    empty = jnp.zeros((1, width), jnp.float32)
    up_next = jnp.concatenate([upward[1:], empty], axis=0)
    down_next = jnp.concatenate([downward[1:], empty], axis=0)
    heat = upward - up_next - (downward - down_next)
    slots = start + jnp.arange(width, dtype=jnp.int32)
    heat = jnp.where(slots[None, :] < count, heat, jnp.zeros_like(heat))
    return heat.astype(jnp.bfloat16)

def reference(grid, legendre, counts, blocks, interp, source_weights, inverses):
    table = dft_table(LON, M)
    fourier = jnp.dot(grid.reshape(FIELDS * LEV * LAT, LON), table, preferred_element_type=jnp.float32)
    fourier = fourier.astype(jnp.bfloat16).reshape(FIELDS, LEV, LAT, M, 2)
    fourier = jnp.transpose(fourier, (3, 0, 1, 2, 4))

    def legendre_one(pair):
        data, weights = pair
        out = jnp.einsum('flar,an->rfln', data.astype(jnp.float32), weights.astype(jnp.float32))
        return out.astype(jnp.bfloat16)
    spectral = lax.map(legendre_one, (fourier, legendre))
    patches = grid.reshape(FIELDS, LEV, N_BAND, NBLK, 128)
    patches = jnp.transpose(patches, (2, 0, 1, 3, 4))
    band_blocks = blocks.reshape(N_BAND, CAP)
    band_weights = interp.reshape(N_BAND, CAP, 128)

    def band_one(item):
        patch, chosen, weights, count = item
        picked = jnp.take(patch, chosen, axis=2)
        state = jnp.einsum('fljk,jk->flj', picked.astype(jnp.float32), weights.astype(jnp.float32))
        state = state.astype(jnp.bfloat16).reshape(FIELDS * LEV, CAP)
        gates = jnp.dot(source_weights.T, state, preferred_element_type=jnp.float32)
        source = jax.nn.softplus(gates).astype(jnp.bfloat16).reshape(BANDS, FLUX, CAP)
        flux = jnp.einsum('bpq,bqj->pj', inverses.astype(jnp.float32), source.astype(jnp.float32))
        heat = heat_rates(flux, count, jnp.int32(0))
        spread = heat.astype(jnp.float32)[:, :, None] * weights.astype(jnp.float32)[None, :, :]
        summed = jax.ops.segment_sum(jnp.transpose(spread, (1, 0, 2)), chosen, num_segments=NBLK)
        return jnp.transpose(summed, (1, 0, 2)).reshape(LEV, LAT_DEV, LON).astype(jnp.bfloat16)
    heating = lax.map(band_one, (patches, band_blocks, band_weights, counts))
    heating = jnp.transpose(heating, (1, 0, 2, 3)).reshape(LEV, LAT, LON)
    return (spectral, heating)
```

```python
import functools
import math

import jax
import jax.numpy as jnp
import ml_dtypes
import numpy as np
from jax import lax
from jax.experimental import pallas as pl
from jax.experimental.pallas import tpu as pltpu
from jax.sharding import PartitionSpec as P

MESH = pl.DeviceIdType.MESH
N_BAND = 32
N_Z = 8
CHUNKS = 3


def dft_table(lon, wave_dev, n_fld):
    waves = wave_dev * N_BAND * n_fld
    per_chunk = wave_dev // CHUNKS
    place = np.arange(lon, dtype=np.int64)
    wave = np.zeros((CHUNKS, 2, 2, n_fld, per_chunk, 2, 8), np.int64)
    part = np.zeros_like(wave)
    c, h, t, f, m, r, i = np.indices(wave.shape)
    band = (h * 2 + t) * 8 + i
    wave = (band * n_fld + f) * wave_dev + c * per_chunk + m
    part = r
    wave = wave.reshape(CHUNKS * 2, 256)
    part = part.reshape(CHUNKS * 2, 256)
    phase = (place[None, :, None] * wave[:, None, :]) % lon
    angle = phase.astype(np.float32) * np.float32(2.0 * math.pi / lon)
    values = np.where(part[:, None, :] == 0, np.cos(angle), -np.sin(angle))
    return (values.astype(np.float32) * np.float32(1.0 / math.sqrt(lon))).astype(ml_dtypes.bfloat16)


def transpose_levels(rows):
    lane = lax.broadcasted_iota(jnp.int32, rows[0].shape, 1)
    for bit in (1, 2, 4):
        high = (lane & bit) != 0
        out = list(rows)
        for l in range(8):
            if l & bit:
                continue
            a, b = rows[l], rows[l + bit]
            out[l] = jnp.where(high, pltpu.roll(b, bit, 1), a)
            out[l + bit] = jnp.where(high, b, pltpu.roll(a, 128 - bit, 1))
        rows = out
    return rows


def kernel(
    grid_hbm, tab_hbm, leg_hbm, out_ref,
    g, tab, leg, send, recv, zsend, zrecv,
    load_sem, bs_sem, br_sem, zs_sem, zr_sem, rs_sem, rr_sem,
):
    lat = send.shape[2]
    band = lax.axis_index("band")
    z = lax.axis_index("fld") * 2 + lax.axis_index("sec")
    sign = 1 - 2 * lax.rem(z, 2)

    def zdev(step):
        at = lax.rem(z + step + 2 * N_Z, N_Z)
        return at, {"sec": lax.rem(at, 2), "fld": at // 2}

    partner, partner_dev = zdev(sign)

    def load_tab(t):
        return pltpu.make_async_copy(tab_hbm.at[t], tab.at[t], load_sem.at[t])

    def load_leg(c):
        return pltpu.make_async_copy(
            leg_hbm.at[pl.ds(2 * c, 2)], leg.at[pl.ds(2 * c, 2)], load_sem.at[7 + c]
        )

    half0 = band // 16
    load_g = pltpu.make_async_copy(grid_hbm, g, load_sem.at[6])
    load_g.start()
    load_tab(half0).start()

    barrier = pltpu.get_barrier_semaphore()

    def greet(k, _):
        pl.semaphore_signal(
            barrier, inc=1, device_id={"band": lax.rem(band + k, N_BAND)}, device_id_type=MESH
        )
        return 0

    lax.fori_loop(1, N_BAND, greet, 0)
    for d in range(1, N_Z):
        pl.semaphore_signal(barrier, inc=1, device_id=zdev(d)[1], device_id_type=MESH)
    load_g.wait()
    pl.semaphore_wait(barrier, N_BAND - 1 + N_Z - 1)

    def band_copy(c, to):
        return pltpu.make_async_remote_copy(
            src_ref=send.at[c, to],
            dst_ref=recv.at[c, band],
            send_sem=bs_sem.at[c],
            recv_sem=br_sem.at[c],
            device_id={"band": to},
            device_id_type=MESH,
        )

    def table_of(t):
        return (t // 2) * 2 + lax.rem(t + half0, 2)

    def dft_step(t, _):
        c = t // 2
        half = lax.rem(t + half0, 2)

        @pl.when(t < 5)
        def _():
            load_tab(table_of(t + 1)).start()

        load_tab(table_of(t)).wait()
        coeffs = jnp.dot(g[...], tab[table_of(t)], preferred_element_type=jnp.float32)
        for tile in range(2):
            rows = [coeffs[l * lat:(l + 1) * lat, tile * 128:(tile + 1) * 128] for l in range(8)]
            rows = transpose_levels(rows)
            for i in range(8):
                send[c, half * 16 + tile * 8 + i] = rows[i].astype(jnp.bfloat16)

        def send_one(k, _):
            to = half * 16 + lax.rem(band + k, 16)

            @pl.when(to != band)
            def _():
                band_copy(c, to).start()

            return 0

        lax.fori_loop(0, 16, send_one, 0)
        return 0

    lax.fori_loop(0, 2 * CHUNKS, dft_step, 0)
    for c in range(CHUNKS):
        load_leg(c).start()

    row = lax.broadcasted_iota(jnp.int32, (128, 128), 0)
    col = lax.broadcasted_iota(jnp.int32, (128, 128), 1)
    eye = (row == col).astype(jnp.bfloat16)

    def own_copy(c):
        return pltpu.make_async_remote_copy(
            src_ref=zsend.at[c, z // 2], dst_ref=zrecv.at[c, z],
            send_sem=zs_sem.at[c, 0], recv_sem=zr_sem.at[c, 0],
            device_id=partner_dev, device_id_type=MESH,
        )

    def direct_copy(c, d):
        at, dev = zdev({1: -sign, 2: 2 * sign, 3: -3 * sign}[d])
        return pltpu.make_async_remote_copy(
            src_ref=zsend.at[c, at // 2], dst_ref=zrecv.at[c, z],
            send_sem=zs_sem.at[c, d], recv_sem=zr_sem.at[c, d],
            device_id=dev, device_id_type=MESH,
        )

    def relay_copy(c, d):
        source, _ = zdev(-d * sign)
        return pltpu.make_async_remote_copy(
            src_ref=zrecv.at[c, source], dst_ref=zrecv.at[c, source],
            send_sem=rs_sem.at[c, d - 1], recv_sem=rr_sem.at[c, d - 1],
            device_id=partner_dev, device_id_type=MESH,
        )

    def turn(c):
        recv[c, band] = send[c, band]
        got = recv.at[c, pl.ds(0, N_BAND - 1)]
        pltpu.make_async_copy(got, got, br_sem.at[c]).wait()
        half = N_BAND // 2
        for part in range(2):
            rows = recv[c, part * half:(part + 1) * half].astype(jnp.float32).reshape(half * lat, 128)
            turned = lax.dot_general(
                eye, rows.astype(jnp.bfloat16), (((1,), (1,)), ((), ())),
                preferred_element_type=jnp.float32,
            ).astype(jnp.bfloat16)
            zsend[c, :, :, part * half * lat:(part + 1) * half * lat] = turned.reshape(4, 32, half * lat)
        for d in (3, 2, 1):
            direct_copy(c, d).start()
        own_copy(c).start()
        zrecv[c, z] = zsend[c, z // 2]

    def relay(c):
        for d in (1, 2, 3):
            direct_copy(c, d).wait_recv()
            relay_copy(c, d).start()

    def legendre(c):
        own_copy(c).wait_recv()
        for d in (1, 2, 3):
            relay_copy(c, d).wait_recv()
        load_leg(c).wait()

        def one(m, _):
            rows = pl.ds(pl.multiple_of(m * 16, 16), 16)
            data = zrecv[c, :, rows, :].reshape(128, zrecv.shape[3])
            out = jnp.dot(data, leg[2 * c + m], preferred_element_type=jnp.float32)
            out = out.reshape(4, 2, 2, 8, out.shape[1])
            for r in range(2):
                for f in range(4):
                    both = jnp.concatenate([out[f, 0, r], out[f, 1, r]], axis=0)
                    out_ref[2 * c + m, r, f] = both.astype(jnp.bfloat16)
            return 0

        lax.fori_loop(0, 2, one, 0)

    turn(0)
    turn(1)
    relay(0)
    turn(2)
    relay(1)
    legendre(0)
    relay(2)
    legendre(1)
    legendre(2)

    for c in range(CHUNKS):
        sent = send.at[c, pl.ds(0, N_BAND - 1)]
        pltpu.make_async_copy(sent, sent, bs_sem.at[c]).wait()
        own_copy(c).wait_send()
        for d in (1, 2, 3):
            direct_copy(c, d).wait_send()
            relay_copy(c, d).wait_send()


def spectral_part(grid, legendre):
    lev_s, lat_d, lon = grid.shape[1:]
    wave_dev, lats, degrees = legendre.shape
    n_fld = lax.axis_size("fld")
    table = jnp.asarray(dft_table(lon, wave_dev, n_fld))
    flat = grid.reshape(lev_s * lat_d, lon)
    bf16 = jnp.bfloat16
    return pl.pallas_call(
        kernel,
        out_shape=jax.ShapeDtypeStruct((wave_dev, 2, n_fld, 2 * lev_s, degrees), bf16),
        in_specs=[pl.BlockSpec(memory_space=pl.ANY)] * 3,
        out_specs=pl.BlockSpec(memory_space=pltpu.VMEM),
        scratch_shapes=[
            pltpu.VMEM(flat.shape, bf16),
            pltpu.VMEM(table.shape, bf16),
            pltpu.VMEM(legendre.shape, bf16),
            pltpu.VMEM((CHUNKS, N_BAND, lat_d, 128), bf16),
            pltpu.VMEM((CHUNKS, N_BAND, lat_d, 128), bf16),
            pltpu.VMEM((CHUNKS, n_fld, 32, lats), bf16),
            pltpu.VMEM((CHUNKS, N_Z, 32, lats), bf16),
            pltpu.SemaphoreType.DMA((10,)),
            pltpu.SemaphoreType.DMA((CHUNKS,)),
            pltpu.SemaphoreType.DMA((CHUNKS,)),
            pltpu.SemaphoreType.DMA((CHUNKS, 4)),
            pltpu.SemaphoreType.DMA((CHUNKS, 4)),
            pltpu.SemaphoreType.DMA((CHUNKS, 3)),
            pltpu.SemaphoreType.DMA((CHUNKS, 3)),
        ],
        compiler_params=pltpu.CompilerParams(
            collective_id=0, has_side_effects=True, vmem_limit_bytes=48 * 2**20
        ),
    )(flat, table, legendre)


def heat_rates(flux, count, start):
    levels = flux.shape[0] // 2
    width = flux.shape[1]
    upward = flux[:levels]
    downward = flux[levels:]
    empty = jnp.zeros((1, width), jnp.float32)
    up_next = jnp.concatenate([upward[1:], empty], axis=0)
    down_next = jnp.concatenate([downward[1:], empty], axis=0)
    heat = upward - up_next - (downward - down_next)
    slots = start + jnp.arange(width, dtype=jnp.int32)
    heat = jnp.where(slots[None, :] < count, heat, jnp.zeros_like(heat))
    return heat.astype(jnp.bfloat16)


def heating_part(grid, counts, blocks, interp, source_weights, inverses):
    n_sec = lax.axis_size("sec")
    n_band = lax.axis_size("band")
    n_fld = lax.axis_size("fld")
    lev_s = grid.shape[1]
    lat_d = grid.shape[2]
    lon = grid.shape[3]
    groups = n_sec * n_fld
    slots_all = blocks.shape[0]
    width = interp.shape[1]
    nblocks = lat_d * lon // width
    patch = grid.reshape(lev_s, nblocks, width)
    block_ids = jnp.arange(nblocks, dtype=jnp.int32)
    selector = (blocks[:, None] == block_ids[None, :]).astype(jnp.bfloat16)
    picked = lax.dot_general(
        selector, patch, (((1,), (1,)), ((), ())), preferred_element_type=jnp.float32
    )
    picked = picked.astype(jnp.bfloat16)
    partial_state = jnp.einsum("jlk,jk->lj", picked, interp, preferred_element_type=jnp.float32)
    partial_state = partial_state.astype(jnp.bfloat16).reshape(1, lev_s, slots_all)
    columns = lax.all_to_all(partial_state, ("sec", "fld"), split_axis=2, concat_axis=0, tiled=True)
    per_dev = slots_all // groups
    state = columns.reshape(n_sec, n_fld, lev_s, per_dev)
    state = jnp.transpose(state, (1, 0, 2, 3)).reshape(n_fld * n_sec * lev_s, per_dev)
    gates = lax.dot_general(
        source_weights, state, (((0,), (0,)), ((), ())), preferred_element_type=jnp.float32
    )
    spec_bands = inverses.shape[0]
    flux_rows = inverses.shape[1]
    source = jax.nn.softplus(gates).astype(jnp.bfloat16).reshape(spec_bands, flux_rows, per_dev)
    flux = jnp.einsum("bpq,bqj->pj", inverses, source, preferred_element_type=jnp.float32)
    band_place = lax.axis_index("band")
    count = jnp.sum(
        jnp.where(jnp.arange(n_band, dtype=jnp.int32) == band_place, counts, jnp.zeros_like(counts))
    )
    group_place = lax.axis_index(("sec", "fld"))
    heat = heat_rates(flux, count, group_place * per_dev)
    returned = lax.all_to_all(heat, ("sec", "fld"), split_axis=0, concat_axis=1, tiled=True)
    spread = (
        jnp.transpose(returned.astype(jnp.float32))[:, :, None]
        * interp.astype(jnp.float32)[:, None, :]
    )
    spread_high = spread.astype(jnp.bfloat16)
    spread_low = (spread - spread_high.astype(jnp.float32)).astype(jnp.bfloat16)
    summed = lax.dot_general(
        selector, spread_high, (((0,), (0,)), ((), ())), preferred_element_type=jnp.float32
    )
    summed = summed + lax.dot_general(
        selector, spread_low, (((0,), (0,)), ((), ())), preferred_element_type=jnp.float32
    )
    return jnp.transpose(summed, (1, 0, 2)).reshape(returned.shape[0], lat_d, lon).astype(jnp.bfloat16)


def body(grid, legendre, counts, blocks, interp, source_weights, inverses):
    spectral = spectral_part(grid, legendre)
    heating = heating_part(grid, counts, blocks, interp, source_weights, inverses)
    return (spectral, heating)


def solution(mesh):
    return jax.shard_map(
        body,
        mesh=mesh,
        in_specs=(
            P("fld", "sec", "band", None),
            P(("band", "fld"), None, "sec"),
            P(),
            P("band"),
            P("band", None),
            P(),
            P(),
        ),
        out_specs=(P(("band", "fld"), None, None, None, "sec"), P(("sec", "fld"), "band", None)),
        check_vma=False,
    )
```

```python
import functools
import math

import jax
import jax.numpy as jnp
import ml_dtypes
import numpy as np
from jax import lax
from jax.experimental import pallas as pl
from jax.experimental.pallas import tpu as pltpu
from jax.sharding import PartitionSpec as P

MESH = pl.DeviceIdType.MESH
N_BAND = 32
N_Z = 8
CHUNKS = 3
PATCH_ROWS = 896


def dft_table(lon, wave_dev, n_fld):
    waves = wave_dev * N_BAND * n_fld
    per_chunk = wave_dev // CHUNKS
    place = np.arange(lon, dtype=np.int64)
    wave = np.zeros((CHUNKS, 2, 2, n_fld, per_chunk, 2, 8), np.int64)
    part = np.zeros_like(wave)
    c, h, t, f, m, r, i = np.indices(wave.shape)
    band = (h * 2 + t) * 8 + i
    wave = (band * n_fld + f) * wave_dev + c * per_chunk + m
    part = r
    wave = wave.reshape(CHUNKS * 2, 256)
    part = part.reshape(CHUNKS * 2, 256)
    phase = (place[None, :, None] * wave[:, None, :]) % lon
    angle = phase.astype(np.float32) * np.float32(2.0 * math.pi / lon)
    values = np.where(part[:, None, :] == 0, np.cos(angle), -np.sin(angle))
    return (values.astype(np.float32) * np.float32(1.0 / math.sqrt(lon))).astype(ml_dtypes.bfloat16)


def transpose_levels(rows):
    lane = lax.broadcasted_iota(jnp.int32, rows[0].shape, 1)
    for bit in (1, 2, 4):
        high = (lane & bit) != 0
        out = list(rows)
        for l in range(8):
            if l & bit:
                continue
            a, b = rows[l], rows[l + bit]
            out[l] = jnp.where(high, pltpu.roll(b, bit, 1), a)
            out[l + bit] = jnp.where(high, b, pltpu.roll(a, 128 - bit, 1))
        rows = out
    return rows


def kernel(
    grid_hbm, tab_hbm, leg_hbm, counts_hbm, blocks_hbm, interp_hbm, weights_hbm, inverse_hbm,
    out_ref, heat_ref,
    g, tab, leg, send, recv, zsend, zrecv,
    counts, blocks, interp, weights, inverse,
    ids, patch, inverse_wide, source, state_send, state_recv, heat_send, heat_recv,
    load_sem, bs_sem, br_sem, zs_sem, zr_sem, rs_sem, rr_sem, small_sem, col_sem,
):
    lat = send.shape[2]
    band = lax.axis_index("band")
    z = lax.axis_index("fld") * 2 + lax.axis_index("sec")
    sign = 1 - 2 * lax.rem(z, 2)

    def zdev(step):
        at = lax.rem(z + step + 2 * N_Z, N_Z)
        return at, {"sec": lax.rem(at, 2), "fld": at // 2}

    partner, partner_dev = zdev(sign)

    def load_tab(t):
        return pltpu.make_async_copy(tab_hbm.at[t], tab.at[t], load_sem.at[t])

    def load_leg(c):
        return pltpu.make_async_copy(
            leg_hbm.at[pl.ds(2 * c, 2)], leg.at[pl.ds(2 * c, 2)], load_sem.at[7 + c]
        )

    half0 = band // 16
    load_g = pltpu.make_async_copy(grid_hbm, g, load_sem.at[6])
    load_g.start()
    load_tab(half0).start()

    barrier = pltpu.get_barrier_semaphore()

    def greet(k, _):
        pl.semaphore_signal(
            barrier, inc=1, device_id={"band": lax.rem(band + k, N_BAND)}, device_id_type=MESH
        )
        return 0

    lax.fori_loop(1, N_BAND, greet, 0)
    for d in range(1, N_Z):
        pl.semaphore_signal(barrier, inc=1, device_id=zdev(d)[1], device_id_type=MESH)
    load_g.wait()
    pl.semaphore_wait(barrier, N_BAND - 1 + N_Z - 1)

    def band_copy(c, to):
        return pltpu.make_async_remote_copy(
            src_ref=send.at[c, to],
            dst_ref=recv.at[c, band],
            send_sem=bs_sem.at[c],
            recv_sem=br_sem.at[c],
            device_id={"band": to},
            device_id_type=MESH,
        )

    def table_of(t):
        return (t // 2) * 2 + lax.rem(t + half0, 2)

    def dft_step(t, _):
        c = t // 2
        half = lax.rem(t + half0, 2)

        @pl.when(t < 5)
        def _():
            load_tab(table_of(t + 1)).start()

        load_tab(table_of(t)).wait()
        coeffs = jnp.dot(g[...], tab[table_of(t)], preferred_element_type=jnp.float32)
        for tile in range(2):
            rows = [coeffs[l * lat:(l + 1) * lat, tile * 128:(tile + 1) * 128] for l in range(8)]
            rows = transpose_levels(rows)
            for i in range(8):
                send[c, half * 16 + tile * 8 + i] = rows[i].astype(jnp.bfloat16)

        def send_one(k, _):
            to = half * 16 + lax.rem(band + k, 16)

            @pl.when(to != band)
            def _():
                band_copy(c, to).start()

            return 0

        lax.fori_loop(0, 16, send_one, 0)
        return 0

    lax.fori_loop(0, 2 * CHUNKS, dft_step, 0)
    small = [
        pltpu.make_async_copy(source_ref, target_ref, small_sem.at[i])
        for i, (source_ref, target_ref) in enumerate(
            ((blocks_hbm, blocks), (interp_hbm, interp), (weights_hbm, weights),
             (inverse_hbm, inverse), (counts_hbm, counts))
        )
    ]
    for load in small:
        load.start()
    for c in range(CHUNKS):
        load_leg(c).start()

    row = lax.broadcasted_iota(jnp.int32, (128, 128), 0)
    col = lax.broadcasted_iota(jnp.int32, (128, 128), 1)
    eye = (row == col).astype(jnp.bfloat16)

    def own_copy(c):
        return pltpu.make_async_remote_copy(
            src_ref=zsend.at[c, z // 2], dst_ref=zrecv.at[c, z],
            send_sem=zs_sem.at[c, 0], recv_sem=zr_sem.at[c, 0],
            device_id=partner_dev, device_id_type=MESH,
        )

    def direct_copy(c, d):
        at, dev = zdev({1: -sign, 2: 2 * sign, 3: -3 * sign}[d])
        return pltpu.make_async_remote_copy(
            src_ref=zsend.at[c, at // 2], dst_ref=zrecv.at[c, z],
            send_sem=zs_sem.at[c, d], recv_sem=zr_sem.at[c, d],
            device_id=dev, device_id_type=MESH,
        )

    def relay_copy(c, d):
        source, _ = zdev(-d * sign)
        return pltpu.make_async_remote_copy(
            src_ref=zrecv.at[c, source], dst_ref=zrecv.at[c, source],
            send_sem=rs_sem.at[c, d - 1], recv_sem=rr_sem.at[c, d - 1],
            device_id=partner_dev, device_id_type=MESH,
        )

    def turn(c):
        recv[c, band] = send[c, band]
        got = recv.at[c, pl.ds(0, N_BAND - 1)]
        pltpu.make_async_copy(got, got, br_sem.at[c]).wait()
        half = N_BAND // 2
        for part in range(2):
            rows = recv[c, part * half:(part + 1) * half].astype(jnp.float32).reshape(half * lat, 128)
            turned = lax.dot_general(
                eye, rows.astype(jnp.bfloat16), (((1,), (1,)), ((), ())),
                preferred_element_type=jnp.float32,
            ).astype(jnp.bfloat16)
            zsend[c, :, :, part * half * lat:(part + 1) * half * lat] = turned.reshape(4, 32, half * lat)
        for d in (3, 2, 1):
            direct_copy(c, d).start()
        own_copy(c).start()
        zrecv[c, z] = zsend[c, z // 2]

    def relay(c):
        for d in (1, 2, 3):
            direct_copy(c, d).wait_recv()
            relay_copy(c, d).start()

    def legendre(c):
        own_copy(c).wait_recv()
        for d in (1, 2, 3):
            relay_copy(c, d).wait_recv()
        load_leg(c).wait()

        def one(m, _):
            rows = pl.ds(pl.multiple_of(m * 16, 16), 16)
            data = zrecv[c, :, rows, :].reshape(128, zrecv.shape[3])
            out = jnp.dot(data, leg[2 * c + m], preferred_element_type=jnp.float32)
            out = out.reshape(4, 2, 2, 8, out.shape[1])
            for r in range(2):
                for f in range(4):
                    both = jnp.concatenate([out[f, 0, r], out[f, 1, r]], axis=0)
                    out_ref[2 * c + m, r, f] = both.astype(jnp.bfloat16)
            return 0

        lax.fori_loop(0, 2, one, 0)

    n_tiles = g.shape[1] // 128
    pairs = (n_tiles + 1) // 2
    pair_rows = 2 * lat

    def block_patch():
        def tile_rows(t):
            cols = pl.ds(pl.multiple_of(t * 128, 128), 128)
            return g[:, cols].astype(jnp.float32)

        def put(u, first, second):
            rows = pl.ds(pl.multiple_of(u * pair_rows, 16), pair_rows)
            for l in range(8):
                span = slice(l * lat, (l + 1) * lat)
                both = jnp.concatenate([first[span], second[span]], axis=0)
                patch[rows, l * 128:(l + 1) * 128] = both.astype(jnp.bfloat16)

        def one(u, _):
            put(u, tile_rows(2 * u), tile_rows(2 * u + 1))
            return 0

        lax.fori_loop(0, n_tiles // 2, one, 0)
        if n_tiles % 2:
            last = tile_rows(n_tiles - 1)
            put(n_tiles // 2, last, jnp.zeros_like(last))
        end = pairs * pair_rows
        patch[end:, :] = jnp.zeros((PATCH_ROWS - end, patch.shape[1]), jnp.bfloat16)
        small[0].wait()
        chosen = blocks[...].astype(jnp.float32)
        at_lat = jnp.floor((chosen + 0.5) * (1.0 / n_tiles))
        ids[...] = (chosen - at_lat * n_tiles) * lat + at_lat

    def column_copy(kind, to, from_buf, to_buf):
        return pltpu.make_async_remote_copy(
            src_ref=from_buf.at[to], dst_ref=to_buf.at[z],
            send_sem=col_sem.at[2 * kind], recv_sem=col_sem.at[2 * kind + 1],
            device_id={"sec": lax.rem(to, 2), "fld": to // 2}, device_id_type=MESH,
        )

    def column_wait(kind, is_recv, buf):
        part = buf.at[pl.ds(0, N_Z - 1)]
        pltpu.make_async_copy(part, part, col_sem.at[2 * kind + is_recv]).wait()

    def gather_state():
        small[1].wait()
        lane = lax.broadcasted_iota(jnp.int32, (128, 128), 1)
        level_of = lax.broadcasted_iota(jnp.int32, (8, 1024), 1) // 128
        ones = (lax.broadcasted_iota(jnp.int32, (8, 1024), 0) == level_of).astype(jnp.bfloat16)

        def one(k, _):
            to = lax.rem(z + k, N_Z)
            want = jnp.transpose(jnp.broadcast_to(ids[pl.ds(to, 1), :], (128, 128)))
            hot = jnp.concatenate(
                [(want == (lane + 128 * i).astype(jnp.float32)).astype(jnp.bfloat16)
                 for i in range(PATCH_ROWS // 128)],
                axis=1,
            )
            picked = jnp.dot(hot, patch[...], preferred_element_type=jnp.float32)
            slot = pl.ds(pl.multiple_of(to * 128, 128), 128)
            factor = interp[slot, :].astype(jnp.float32)
            terms = picked * jnp.concatenate([factor] * 8, axis=1)
            high = terms.astype(jnp.bfloat16)
            low = (terms - high.astype(jnp.float32)).astype(jnp.bfloat16)
            contract = (((1,), (1,)), ((), ()))
            state_send[to] = lax.dot_general(
                ones, high, contract, preferred_element_type=jnp.float32
            ) + lax.dot_general(ones, low, contract, preferred_element_type=jnp.float32)

            @pl.when(to != z)
            def _():
                column_copy(0, to, state_send, state_recv).start()

            return 0

        lax.fori_loop(1, N_Z + 1, one, 0)

    def solve_columns():
        small[2].wait()
        small[3].wait()
        small[4].wait()
        inverse_wide[...] = inverse[...].astype(jnp.float32)
        state_recv[z] = state_send[z]
        column_wait(0, 1, state_recv)
        state = state_recv[...].reshape(64, 128).astype(jnp.bfloat16)

        def sources(i, _):
            cols = pl.ds(pl.multiple_of(i * 256, 256), 256)
            gates = lax.dot_general(
                weights[:, cols], state, (((0,), (0,)), ((), ())), preferred_element_type=jnp.float32
            )
            source[cols, :] = jax.nn.softplus(gates)
            return 0

        lax.fori_loop(0, weights.shape[1] // 256, sources, 0)
        spec_bands = inverse.shape[1]
        flux_rows = inverse.shape[0] // 32

        def fluxes(q, total):
            factor = inverse_wide[pl.ds(q, 32, stride=32), :].astype(jnp.bfloat16)
            value = source[pl.ds(q, spec_bands, stride=32), :].astype(jnp.bfloat16)
            return total + jnp.dot(factor, value, preferred_element_type=jnp.float32)

        flux = lax.fori_loop(0, flux_rows, fluxes, jnp.zeros((32, 128), jnp.float32))
        row16 = lax.broadcasted_iota(jnp.int32, (16, 128), 0)

        def drop(rows):
            above = jnp.where(row16 < 15, pltpu.roll(rows, 15, 0), 0.0)
            return rows - above

        heat = drop(flux[:16]) - drop(flux[16:])
        slot = (z * 128 + lax.broadcasted_iota(jnp.int32, (1, 128), 1)).astype(jnp.float32)
        at = lax.broadcasted_iota(jnp.int32, (1, N_BAND), 1)
        live = jnp.sum(
            jnp.where(at == band, counts[...].astype(jnp.float32), 0.0), axis=1, keepdims=True
        )
        heat = jnp.where(slot < live, heat, 0.0)
        heat = heat.astype(jnp.bfloat16).astype(jnp.float32)
        for group in range(N_Z):
            rows = heat[(group // 4) * 8:(group // 4) * 8 + 8]
            shift = (8 - 2 * (group % 4)) % 8
            heat_send[2 * (group % 4) + group // 4] = pltpu.roll(rows, shift, 0) if shift else rows

        def send_heat(k, _):
            column_copy(1, lax.rem(z + k, N_Z), heat_send, heat_recv).start()
            return 0

        lax.fori_loop(1, N_Z, send_heat, 0)

    def scatter_heat():
        heat_recv[z] = heat_send[z]
        column_wait(1, 1, heat_recv)
        step = lax.broadcasted_iota(jnp.int32, (pair_rows, 128), 0)

        def one(u, _):
            row = (step + u * pair_rows).astype(jnp.float32)
            parts = [[], []]
            for place in range(N_Z):
                hit = ids[place:place + 1, :] == row
                for l in range(2):
                    parts[l].append(
                        jnp.where(hit, heat_recv[place, l:l + 1, :], 0.0).astype(jnp.bfloat16)
                    )
            rows = jnp.concatenate([jnp.concatenate(p, axis=1) for p in parts], axis=0)
            summed = jnp.dot(rows, interp[...], preferred_element_type=jnp.float32)
            for l in range(2):
                for t in range(2):
                    value = summed[l * pair_rows + t * lat:l * pair_rows + (t + 1) * lat]
                    cols = pl.ds(pl.multiple_of((2 * u + t) * 128, 128), 128)

                    def put():
                        heat_ref[l, :, cols] = value.astype(jnp.bfloat16)

                    if t == 0:
                        put()
                    else:
                        pl.when(2 * u + 1 < n_tiles)(put)
            return 0

        lax.fori_loop(0, pairs, one, 0)

    turn(0)
    block_patch()
    turn(1)
    gather_state()
    relay(0)
    turn(2)
    solve_columns()
    relay(1)
    legendre(0)
    scatter_heat()
    relay(2)
    legendre(1)
    legendre(2)

    column_wait(0, 0, state_send)
    column_wait(1, 0, heat_send)
    for c in range(CHUNKS):
        sent = send.at[c, pl.ds(0, N_BAND - 1)]
        pltpu.make_async_copy(sent, sent, bs_sem.at[c]).wait()
        own_copy(c).wait_send()
        for d in (1, 2, 3):
            direct_copy(c, d).wait_send()
            relay_copy(c, d).wait_send()


def body(grid, legendre, counts, blocks, interp, source_weights, inverses):
    lev_s, lat_d, lon = grid.shape[1:]
    wave_dev, lats, degrees = legendre.shape
    n_fld = lax.axis_size("fld")
    n_sec = lax.axis_size("sec")
    slots, width = interp.shape
    rows_in, sources = source_weights.shape
    spec_bands, flux_rows, _ = inverses.shape
    table = jnp.asarray(dft_table(lon, wave_dev, n_fld))
    flat = grid.reshape(lev_s * lat_d, lon)
    inv_rows = jnp.transpose(inverses, (1, 2, 0)).reshape(flux_rows * flux_rows, spec_bands)
    lev_out = n_sec * lev_s // (n_sec * n_fld)
    bf16, f32 = jnp.bfloat16, jnp.float32
    spectral, heating = pl.pallas_call(
        kernel,
        out_shape=(
            jax.ShapeDtypeStruct((wave_dev, 2, n_fld, n_sec * lev_s, degrees), bf16),
            jax.ShapeDtypeStruct((lev_out, lat_d, lon), bf16),
        ),
        in_specs=[pl.BlockSpec(memory_space=pl.ANY)] * 8,
        out_specs=(
            pl.BlockSpec(memory_space=pltpu.VMEM),
            pl.BlockSpec(memory_space=pltpu.VMEM),
        ),
        scratch_shapes=[
            pltpu.VMEM(flat.shape, bf16),
            pltpu.VMEM(table.shape, bf16),
            pltpu.VMEM(legendre.shape, bf16),
            pltpu.VMEM((CHUNKS, N_BAND, lat_d, 128), bf16),
            pltpu.VMEM((CHUNKS, N_BAND, lat_d, 128), bf16),
            pltpu.VMEM((CHUNKS, n_fld, 32, lats), bf16),
            pltpu.VMEM((CHUNKS, N_Z, 32, lats), bf16),
            pltpu.VMEM((1, N_BAND), jnp.int32),
            pltpu.VMEM((N_Z, 128), jnp.int32),
            pltpu.VMEM(interp.shape, bf16),
            pltpu.VMEM(source_weights.shape, bf16),
            pltpu.VMEM(inv_rows.shape, bf16),
            pltpu.VMEM((N_Z, 128), f32),
            pltpu.VMEM((PATCH_ROWS, lev_s * width), bf16),
            pltpu.VMEM(inv_rows.shape, f32),
            pltpu.VMEM((sources, 128), f32),
            pltpu.VMEM((N_Z, 8, 128), f32),
            pltpu.VMEM((N_Z, 8, 128), f32),
            pltpu.VMEM((N_Z, 8, 128), f32),
            pltpu.VMEM((N_Z, 8, 128), f32),
            pltpu.SemaphoreType.DMA((10,)),
            pltpu.SemaphoreType.DMA((CHUNKS,)),
            pltpu.SemaphoreType.DMA((CHUNKS,)),
            pltpu.SemaphoreType.DMA((CHUNKS, 4)),
            pltpu.SemaphoreType.DMA((CHUNKS, 4)),
            pltpu.SemaphoreType.DMA((CHUNKS, 3)),
            pltpu.SemaphoreType.DMA((CHUNKS, 3)),
            pltpu.SemaphoreType.DMA((5,)),
            pltpu.SemaphoreType.DMA((4,)),
        ],
        compiler_params=pltpu.CompilerParams(
            collective_id=0, has_side_effects=True, vmem_limit_bytes=48 * 2**20
        ),
    )(
        flat, table, legendre, counts.reshape(1, N_BAND), blocks.reshape(N_Z, 128), interp,
        source_weights, inv_rows,
    )
    return (spectral, heating)


def solution(mesh):
    return jax.shard_map(
        body,
        mesh=mesh,
        in_specs=(
            P("fld", "sec", "band", None),
            P(("band", "fld"), None, "sec"),
            P(),
            P("band"),
            P("band", None),
            P(),
            P(),
        ),
        out_specs=(P(("band", "fld"), None, None, None, "sec"), P(("sec", "fld"), "band", None)),
        check_vma=False,
    )
```

```python
import functools
import math

import jax
import jax.numpy as jnp
import ml_dtypes
import numpy as np
from jax import lax
from jax.experimental import pallas as pl
from jax.experimental.pallas import tpu as pltpu
from jax.sharding import PartitionSpec as P

MESH = pl.DeviceIdType.MESH
N_BAND = 32
N_Z = 8
CHUNKS = 3
PATCH_ROWS = 896


def dft_table(lon, wave_dev, n_fld):
    waves = wave_dev * N_BAND * n_fld
    per_chunk = wave_dev // CHUNKS
    place = np.arange(lon, dtype=np.int64)
    wave = np.zeros((CHUNKS, 2, 2, n_fld, per_chunk, 2, 8), np.int64)
    part = np.zeros_like(wave)
    c, h, t, f, m, r, i = np.indices(wave.shape)
    band = (h * 2 + t) * 8 + i
    wave = (band * n_fld + f) * wave_dev + c * per_chunk + m
    part = r
    wave = wave.reshape(CHUNKS * 2, 256)
    part = part.reshape(CHUNKS * 2, 256)
    phase = (place[None, :, None] * wave[:, None, :]) % lon
    angle = phase.astype(np.float32) * np.float32(2.0 * math.pi / lon)
    values = np.where(part[:, None, :] == 0, np.cos(angle), -np.sin(angle))
    return (values.astype(np.float32) * np.float32(1.0 / math.sqrt(lon))).astype(ml_dtypes.bfloat16)


def transpose_levels(rows):
    lane = lax.broadcasted_iota(jnp.int32, rows[0].shape, 1)
    for bit in (1, 2, 4):
        high = (lane & bit) != 0
        out = list(rows)
        for l in range(8):
            if l & bit:
                continue
            a, b = rows[l], rows[l + bit]
            out[l] = jnp.where(high, pltpu.roll(b, bit, 1), a)
            out[l + bit] = jnp.where(high, b, pltpu.roll(a, 128 - bit, 1))
        rows = out
    return rows


def kernel(
    grid_hbm, tab_hbm, leg_hbm, counts_hbm, blocks_hbm, interp_hbm, weights_hbm, inverse_hbm,
    out_ref, heat_ref,
    g, tab, leg, send, recv, zsend, zrecv,
    counts, blocks, interp, weights, inverse,
    ids, patch, hot, inverse_wide, source, state_send, state_recv, heat_send, heat_recv,
    load_sem, bs_sem, br_sem, zs_sem, zr_sem, rs_sem, rr_sem, small_sem, col_sem,
):
    lat = send.shape[2]
    band = lax.axis_index("band")
    z = lax.axis_index("fld") * 2 + lax.axis_index("sec")
    sign = 1 - 2 * lax.rem(z, 2)

    def zdev(step):
        at = lax.rem(z + step + 2 * N_Z, N_Z)
        return at, {"sec": lax.rem(at, 2), "fld": at // 2}

    partner, partner_dev = zdev(sign)

    def load_tab(t):
        return pltpu.make_async_copy(tab_hbm.at[t], tab.at[t], load_sem.at[t])

    def load_leg(c):
        return pltpu.make_async_copy(
            leg_hbm.at[pl.ds(2 * c, 2)], leg.at[pl.ds(2 * c, 2)], load_sem.at[7 + c]
        )

    load_g = pltpu.make_async_copy(grid_hbm, g, load_sem.at[6])
    load_g.start()
    load_tab(0).start()
    load_tab(1).start()

    barrier = pltpu.get_barrier_semaphore()

    def greet(k, _):
        pl.semaphore_signal(
            barrier, inc=1, device_id={"band": lax.rem(band + k, N_BAND)}, device_id_type=MESH
        )
        return 0

    lax.fori_loop(1, N_BAND, greet, 0)
    for d in range(1, N_Z):
        pl.semaphore_signal(barrier, inc=1, device_id=zdev(d)[1], device_id_type=MESH)
    for t in range(2, 2 * CHUNKS):
        load_tab(t).start()
    small = [
        pltpu.make_async_copy(source_ref, target_ref, small_sem.at[i])
        for i, (source_ref, target_ref) in enumerate(
            ((blocks_hbm, blocks), (interp_hbm, interp), (weights_hbm, weights),
             (inverse_hbm, inverse), (counts_hbm, counts))
        )
    ]
    load_g.wait()

    def dft_step(t, _):
        c = t // 2
        load_tab(t).wait()
        coeffs = jnp.dot(g[...], tab[t], preferred_element_type=jnp.float32)
        for tile in range(2):
            rows = [coeffs[l * lat:(l + 1) * lat, tile * 128:(tile + 1) * 128] for l in range(8)]
            rows = transpose_levels(rows)
            for i in range(8):
                send[c, lax.rem(t, 2) * 16 + tile * 8 + i] = rows[i].astype(jnp.bfloat16)
        return 0

    def dft(c):
        lax.fori_loop(2 * c, 2 * c + 2, dft_step, 0)

    def send_bands(c):
        def one(k, _):
            to = lax.rem(band + k, N_BAND)
            pltpu.make_async_remote_copy(
                src_ref=send.at[c, to],
                dst_ref=recv.at[c, band],
                send_sem=bs_sem.at[c],
                recv_sem=br_sem.at[c],
                device_id={"band": to},
                device_id_type=MESH,
            ).start()
            return 0

        lax.fori_loop(1, N_BAND, one, 0)
        recv[c, band] = send[c, band]

    row = lax.broadcasted_iota(jnp.int32, (128, 128), 0)
    col = lax.broadcasted_iota(jnp.int32, (128, 128), 1)
    eye = (row == col).astype(jnp.bfloat16)

    def own_copy(c):
        return pltpu.make_async_remote_copy(
            src_ref=zsend.at[c, z // 2], dst_ref=zrecv.at[c, z],
            send_sem=zs_sem.at[c, 0], recv_sem=zr_sem.at[c, 0],
            device_id=partner_dev, device_id_type=MESH,
        )

    def direct_copy(c, d):
        at, dev = zdev({1: -sign, 2: 2 * sign, 3: -3 * sign}[d])
        return pltpu.make_async_remote_copy(
            src_ref=zsend.at[c, at // 2], dst_ref=zrecv.at[c, z],
            send_sem=zs_sem.at[c, d], recv_sem=zr_sem.at[c, d],
            device_id=dev, device_id_type=MESH,
        )

    def relay_copy(c, d):
        source, _ = zdev(-d * sign)
        return pltpu.make_async_remote_copy(
            src_ref=zrecv.at[c, source], dst_ref=zrecv.at[c, source],
            send_sem=rs_sem.at[c, d - 1], recv_sem=rr_sem.at[c, d - 1],
            device_id=partner_dev, device_id_type=MESH,
        )

    def turn(c):
        got = recv.at[c, pl.ds(0, N_BAND - 1)]
        pltpu.make_async_copy(got, got, br_sem.at[c]).wait()
        half = N_BAND // 2
        for part in range(2):
            rows = recv[c, part * half:(part + 1) * half].astype(jnp.float32).reshape(half * lat, 128)
            turned = lax.dot_general(
                eye, rows.astype(jnp.bfloat16), (((1,), (1,)), ((), ())),
                preferred_element_type=jnp.float32,
            ).astype(jnp.bfloat16)
            zsend[c, :, :, part * half * lat:(part + 1) * half * lat] = turned.reshape(4, 32, half * lat)
        for d in (3, 2, 1):
            direct_copy(c, d).start()
        own_copy(c).start()
        zrecv[c, z] = zsend[c, z // 2]

    def relay(c):
        for d in (1, 2, 3):
            direct_copy(c, d).wait_recv()
            relay_copy(c, d).start()

    def legendre(c):
        own_copy(c).wait_recv()
        for d in (1, 2, 3):
            relay_copy(c, d).wait_recv()
        load_leg(c).wait()

        def one(m, _):
            rows = pl.ds(pl.multiple_of(m * 16, 16), 16)
            data = zrecv[c, :, rows, :].reshape(128, zrecv.shape[3])
            out = jnp.dot(data, leg[2 * c + m], preferred_element_type=jnp.float32)
            out = out.reshape(4, 2, 2, 8, out.shape[1])
            for r in range(2):
                for f in range(4):
                    both = jnp.concatenate([out[f, 0, r], out[f, 1, r]], axis=0)
                    out_ref[2 * c + m, r, f] = both.astype(jnp.bfloat16)
            return 0

        lax.fori_loop(0, 2, one, 0)

    n_tiles = g.shape[1] // 128
    pairs = (n_tiles + 1) // 2
    pair_rows = 2 * lat

    def block_patch():
        def tile_rows(t):
            cols = pl.ds(pl.multiple_of(t * 128, 128), 128)
            return g[:, cols].astype(jnp.float32)

        def put(u, first, second):
            rows = pl.ds(pl.multiple_of(u * pair_rows, 16), pair_rows)
            for l in range(8):
                span = slice(l * lat, (l + 1) * lat)
                both = jnp.concatenate([first[span], second[span]], axis=0)
                patch[rows, l * 128:(l + 1) * 128] = both.astype(jnp.bfloat16)

        def one(u, _):
            put(u, tile_rows(2 * u), tile_rows(2 * u + 1))
            return 0

        lax.fori_loop(0, n_tiles // 2, one, 0)
        if n_tiles % 2:
            last = tile_rows(n_tiles - 1)
            put(n_tiles // 2, last, jnp.zeros_like(last))
        end = pairs * pair_rows
        patch[end:, :] = jnp.zeros((PATCH_ROWS - end, patch.shape[1]), jnp.bfloat16)
        small[0].wait()
        chosen = blocks[...].astype(jnp.float32)
        at_lat = jnp.floor((chosen + 0.5) * (1.0 / n_tiles))
        ids[...] = (chosen - at_lat * n_tiles) * lat + at_lat

    def column_copy(kind, to, from_buf, to_buf):
        return pltpu.make_async_remote_copy(
            src_ref=from_buf.at[to], dst_ref=to_buf.at[z],
            send_sem=col_sem.at[2 * kind], recv_sem=col_sem.at[2 * kind + 1],
            device_id={"sec": lax.rem(to, 2), "fld": to // 2}, device_id_type=MESH,
        )

    def column_wait(kind, is_recv, buf):
        part = buf.at[pl.ds(0, N_Z - 1)]
        pltpu.make_async_copy(part, part, col_sem.at[2 * kind + is_recv]).wait()

    def gather_state():
        small[1].wait()
        lane = lax.broadcasted_iota(jnp.int32, (128, 128), 1)
        row8 = lax.broadcasted_iota(jnp.int32, (8, 256), 0)
        level_of = lax.broadcasted_iota(jnp.int32, (8, 256), 1) // 128
        contract = (((1,), (1,)), ((), ()))
        for half in range(2):
            for k in range(4):
                place = half * 4 + k
                want = jnp.transpose(jnp.broadcast_to(ids[place:place + 1, :], (128, 128)))
                hot[k * 128:(k + 1) * 128, :] = jnp.concatenate(
                    [(want == (lane + 128 * i).astype(jnp.float32)).astype(jnp.bfloat16)
                     for i in range(PATCH_ROWS // 128)],
                    axis=1,
                )

            def two_levels(p, total):
                cols = pl.ds(pl.multiple_of(p * 256, 256), 256)
                picked = jnp.dot(hot[...], patch[:, cols], preferred_element_type=jnp.float32)
                factor = interp[half * 512:(half + 1) * 512, :].astype(jnp.float32)
                terms = picked * jnp.concatenate([factor, factor], axis=1)
                high = terms.astype(jnp.bfloat16)
                low = (terms - high.astype(jnp.float32)).astype(jnp.bfloat16)
                ones = (row8 == level_of + 2 * p).astype(jnp.bfloat16)
                return total + lax.dot_general(
                    ones, high, contract, preferred_element_type=jnp.float32
                ) + lax.dot_general(ones, low, contract, preferred_element_type=jnp.float32)

            total = lax.fori_loop(0, 4, two_levels, jnp.zeros((8, 512), jnp.float32))
            for k in range(4):
                state_send[half * 4 + k] = total[:, k * 128:(k + 1) * 128]

        def send_state(k, _):
            column_copy(0, lax.rem(z + k, N_Z), state_send, state_recv).start()
            return 0

        lax.fori_loop(1, N_Z, send_state, 0)
        state_recv[z] = state_send[z]
        small[2].wait()
        small[3].wait()
        small[4].wait()
        inverse_wide[...] = inverse[...].astype(jnp.float32)

    def solve_columns():
        column_wait(0, 1, state_recv)
        state = state_recv[...].reshape(64, 128).astype(jnp.bfloat16)

        def sources(i, _):
            cols = pl.ds(pl.multiple_of(i * 256, 256), 256)
            gates = lax.dot_general(
                weights[:, cols], state, (((0,), (0,)), ((), ())), preferred_element_type=jnp.float32
            )
            source[cols, :] = jax.nn.softplus(gates)
            return 0

        lax.fori_loop(0, weights.shape[1] // 256, sources, 0)
        spec_bands = inverse.shape[1]
        flux_rows = inverse.shape[0] // 32

        sums = []
        for q in range(flux_rows):
            factor = inverse_wide[pl.ds(q, 32, stride=32), :].astype(jnp.bfloat16)
            value = source[pl.ds(q, spec_bands, stride=32), :].astype(jnp.bfloat16)
            sums.append(jnp.dot(factor, value, preferred_element_type=jnp.float32))
        while len(sums) > 1:
            sums = [first + second for first, second in zip(sums[::2], sums[1::2])]
        flux = sums[0]
        row16 = lax.broadcasted_iota(jnp.int32, (16, 128), 0)

        def drop(rows):
            above = jnp.where(row16 < 15, pltpu.roll(rows, 15, 0), 0.0)
            return rows - above

        heat = drop(flux[:16]) - drop(flux[16:])
        slot = (z * 128 + lax.broadcasted_iota(jnp.int32, (1, 128), 1)).astype(jnp.float32)
        at = lax.broadcasted_iota(jnp.int32, (1, N_BAND), 1)
        live = jnp.sum(
            jnp.where(at == band, counts[...].astype(jnp.float32), 0.0), axis=1, keepdims=True
        )
        heat = jnp.where(slot < live, heat, 0.0)
        heat = heat.astype(jnp.bfloat16).astype(jnp.float32)
        for group in range(N_Z):
            rows = heat[(group // 4) * 8:(group // 4) * 8 + 8]
            shift = (8 - 2 * (group % 4)) % 8
            heat_send[2 * (group % 4) + group // 4] = pltpu.roll(rows, shift, 0) if shift else rows

        def send_heat(k, _):
            column_copy(1, lax.rem(z + k, N_Z), heat_send, heat_recv).start()
            return 0

        lax.fori_loop(1, N_Z, send_heat, 0)

    def scatter_heat():
        heat_recv[z] = heat_send[z]
        column_wait(1, 1, heat_recv)
        step = lax.broadcasted_iota(jnp.int32, (pair_rows, 128), 0)

        def one(u, _):
            row = (step + u * pair_rows).astype(jnp.float32)
            parts = [[], []]
            for place in range(N_Z):
                hit = ids[place:place + 1, :] == row
                for l in range(2):
                    parts[l].append(
                        jnp.where(hit, heat_recv[place, l:l + 1, :], 0.0).astype(jnp.bfloat16)
                    )
            rows = jnp.concatenate([jnp.concatenate(p, axis=1) for p in parts], axis=0)
            summed = jnp.dot(rows, interp[...], preferred_element_type=jnp.float32)
            for l in range(2):
                for t in range(2):
                    value = summed[l * pair_rows + t * lat:l * pair_rows + (t + 1) * lat]
                    cols = pl.ds(pl.multiple_of((2 * u + t) * 128, 128), 128)

                    def put():
                        heat_ref[l, :, cols] = value.astype(jnp.bfloat16)

                    if t == 0:
                        put()
                    else:
                        pl.when(2 * u + 1 < n_tiles)(put)
            return 0

        lax.fori_loop(0, pairs, one, 0)

    dft(0)
    for load in small:
        load.start()
    for c in range(CHUNKS):
        load_leg(c).start()
    pl.semaphore_wait(barrier, N_BAND - 1 + N_Z - 1)
    send_bands(0)
    dft(1)
    send_bands(1)
    block_patch()
    gather_state()
    turn(0)
    dft(2)
    send_bands(2)
    turn(1)
    relay(0)
    turn(2)
    solve_columns()
    relay(1)
    legendre(0)
    relay(2)
    legendre(1)
    scatter_heat()
    legendre(2)

    column_wait(0, 0, state_send)
    column_wait(1, 0, heat_send)
    for c in range(CHUNKS):
        sent = send.at[c, pl.ds(0, N_BAND - 1)]
        pltpu.make_async_copy(sent, sent, bs_sem.at[c]).wait()
        own_copy(c).wait_send()
        for d in (1, 2, 3):
            direct_copy(c, d).wait_send()
            relay_copy(c, d).wait_send()


def body(grid, legendre, counts, blocks, interp, source_weights, inverses):
    lev_s, lat_d, lon = grid.shape[1:]
    wave_dev, lats, degrees = legendre.shape
    n_fld = lax.axis_size("fld")
    n_sec = lax.axis_size("sec")
    slots, width = interp.shape
    rows_in, sources = source_weights.shape
    spec_bands, flux_rows, _ = inverses.shape
    table = jnp.asarray(dft_table(lon, wave_dev, n_fld))
    flat = grid.reshape(lev_s * lat_d, lon)
    inv_rows = jnp.transpose(inverses, (1, 2, 0)).reshape(flux_rows * flux_rows, spec_bands)
    lev_out = n_sec * lev_s // (n_sec * n_fld)
    bf16, f32 = jnp.bfloat16, jnp.float32
    spectral, heating = pl.pallas_call(
        kernel,
        out_shape=(
            pltpu.VMEM((wave_dev, 2, n_fld, n_sec * lev_s, degrees), bf16),
            pltpu.VMEM((lev_out, lat_d, lon), bf16),
        ),
        in_specs=[pl.BlockSpec(memory_space=pltpu.HBM)] * 8,
        out_specs=(
            pl.BlockSpec(memory_space=pltpu.VMEM),
            pl.BlockSpec(memory_space=pltpu.VMEM),
        ),
        scratch_shapes=[
            pltpu.VMEM(flat.shape, bf16),
            pltpu.VMEM(table.shape, bf16),
            pltpu.VMEM(legendre.shape, bf16),
            pltpu.VMEM((CHUNKS, N_BAND, lat_d, 128), bf16),
            pltpu.VMEM((CHUNKS, N_BAND, lat_d, 128), bf16),
            pltpu.VMEM((CHUNKS, n_fld, 32, lats), bf16),
            pltpu.VMEM((CHUNKS, N_Z, 32, lats), bf16),
            pltpu.VMEM((1, N_BAND), jnp.int32),
            pltpu.VMEM((N_Z, 128), jnp.int32),
            pltpu.VMEM(interp.shape, bf16),
            pltpu.VMEM(source_weights.shape, bf16),
            pltpu.VMEM(inv_rows.shape, bf16),
            pltpu.VMEM((N_Z, 128), f32),
            pltpu.VMEM((PATCH_ROWS, lev_s * width), bf16),
            pltpu.VMEM((slots // 2, PATCH_ROWS), bf16),
            pltpu.VMEM(inv_rows.shape, f32),
            pltpu.VMEM((sources, 128), f32),
            pltpu.VMEM((N_Z, 8, 128), f32),
            pltpu.VMEM((N_Z, 8, 128), f32),
            pltpu.VMEM((N_Z, 8, 128), f32),
            pltpu.VMEM((N_Z, 8, 128), f32),
            pltpu.SemaphoreType.DMA((10,)),
            pltpu.SemaphoreType.DMA((CHUNKS,)),
            pltpu.SemaphoreType.DMA((CHUNKS,)),
            pltpu.SemaphoreType.DMA((CHUNKS, 4)),
            pltpu.SemaphoreType.DMA((CHUNKS, 4)),
            pltpu.SemaphoreType.DMA((CHUNKS, 3)),
            pltpu.SemaphoreType.DMA((CHUNKS, 3)),
            pltpu.SemaphoreType.DMA((5,)),
            pltpu.SemaphoreType.DMA((4,)),
        ],
        compiler_params=pltpu.CompilerParams(
            collective_id=0, has_side_effects=True, vmem_limit_bytes=62 * 2**20
        ),
    )(
        flat, table, legendre, counts.reshape(1, N_BAND), blocks.reshape(N_Z, 128), interp,
        source_weights, inv_rows,
    )
    return (spectral, heating)


def solution(mesh):
    return jax.shard_map(
        body,
        mesh=mesh,
        in_specs=(
            P("fld", "sec", "band", None),
            P(("band", "fld"), None, "sec"),
            P(),
            P("band"),
            P("band", None),
            P(),
            P(),
        ),
        out_specs=(P(("band", "fld"), None, None, None, "sec"), P(("sec", "fld"), "band", None)),
        check_vma=False,
    )
```

```python
import functools
import math

import jax
import jax.numpy as jnp
import ml_dtypes
import numpy as np
from jax import lax
from jax.experimental import pallas as pl
from jax.experimental.pallas import tpu as pltpu
from jax.sharding import PartitionSpec as P

MESH = pl.DeviceIdType.MESH
N_BAND = 32
N_Z = 8
CHUNKS = 3
PATCH_ROWS = 896


def dft_table(lon, wave_dev, n_fld):
    waves = wave_dev * N_BAND * n_fld
    per_chunk = wave_dev // CHUNKS
    place = np.arange(lon, dtype=np.int64)
    wave = np.zeros((CHUNKS, 2, 2, n_fld, per_chunk, 2, 8), np.int64)
    part = np.zeros_like(wave)
    c, h, t, f, m, r, i = np.indices(wave.shape)
    band = (h * 2 + t) * 8 + i
    wave = (band * n_fld + f) * wave_dev + c * per_chunk + m
    part = r
    wave = wave.reshape(CHUNKS * 2, 256)
    part = part.reshape(CHUNKS * 2, 256)
    phase = (place[None, :, None] * wave[:, None, :]) % lon
    angle = phase.astype(np.float32) * np.float32(2.0 * math.pi / lon)
    values = np.where(part[:, None, :] == 0, np.cos(angle), -np.sin(angle))
    return (values.astype(np.float32) * np.float32(1.0 / math.sqrt(lon))).astype(ml_dtypes.bfloat16)


def transpose_levels(rows):
    lane = lax.broadcasted_iota(jnp.int32, rows[0].shape, 1)
    for bit in (1, 2, 4):
        high = (lane & bit) != 0
        out = list(rows)
        for l in range(8):
            if l & bit:
                continue
            a, b = rows[l], rows[l + bit]
            out[l] = jnp.where(high, pltpu.roll(b, bit, 1), a)
            out[l + bit] = jnp.where(high, b, pltpu.roll(a, 128 - bit, 1))
        rows = out
    return rows


def kernel(
    grid_hbm, tab_hbm, leg_hbm, counts_hbm, blocks_hbm, interp_hbm, weights_hbm, inverse_hbm,
    out_ref, heat_ref,
    g, tab, leg, send, recv, zsend, zrecv,
    counts, blocks, interp, weights, inverse,
    ids, patch, patch_t, interp_t, inverse_wide, source, state_send, state_recv, heat_send, heat_recv,
    load_sem, bs_sem, br_sem, zs_sem, zr_sem, rs_sem, rr_sem, small_sem, col_sem,
):
    lat = send.shape[2]
    band = lax.axis_index("band")
    z = lax.axis_index("fld") * 2 + lax.axis_index("sec")
    sign = 1 - 2 * lax.rem(z, 2)

    def zdev(step):
        at = lax.rem(z + step + 2 * N_Z, N_Z)
        return at, {"sec": lax.rem(at, 2), "fld": at // 2}

    partner, partner_dev = zdev(sign)

    def load_tab(t):
        return pltpu.make_async_copy(tab_hbm.at[t], tab.at[t], load_sem.at[t])

    def load_leg(c):
        return pltpu.make_async_copy(
            leg_hbm.at[pl.ds(2 * c, 2)], leg.at[pl.ds(2 * c, 2)], load_sem.at[7 + c]
        )

    load_g = pltpu.make_async_copy(grid_hbm, g, load_sem.at[6])
    load_g.start()
    load_tab(0).start()
    load_tab(1).start()

    barrier = pltpu.get_barrier_semaphore()

    def greet(k, _):
        pl.semaphore_signal(
            barrier, inc=1, device_id={"band": lax.rem(band + k, N_BAND)}, device_id_type=MESH
        )
        return 0

    lax.fori_loop(1, N_BAND, greet, 0)
    for d in range(1, N_Z):
        pl.semaphore_signal(barrier, inc=1, device_id=zdev(d)[1], device_id_type=MESH)
    for t in range(2, 2 * CHUNKS):
        load_tab(t).start()
    small = [
        pltpu.make_async_copy(source_ref, target_ref, small_sem.at[i])
        for i, (source_ref, target_ref) in enumerate(
            ((blocks_hbm, blocks), (interp_hbm, interp), (weights_hbm, weights),
             (inverse_hbm, inverse), (counts_hbm, counts))
        )
    ]
    load_g.wait()

    def dft_step(t, _):
        c = t // 2
        load_tab(t).wait()
        coeffs = jnp.dot(g[...], tab[t], preferred_element_type=jnp.float32)
        for tile in range(2):
            rows = [coeffs[l * lat:(l + 1) * lat, tile * 128:(tile + 1) * 128] for l in range(8)]
            rows = transpose_levels(rows)
            for i in range(8):
                send[c, lax.rem(t, 2) * 16 + tile * 8 + i] = rows[i].astype(jnp.bfloat16)
        return 0

    def dft(c):
        lax.fori_loop(2 * c, 2 * c + 2, dft_step, 0)

    def send_bands(c):
        def one(k, _):
            to = lax.rem(band + k, N_BAND)
            pltpu.make_async_remote_copy(
                src_ref=send.at[c, to],
                dst_ref=recv.at[c, band],
                send_sem=bs_sem.at[c],
                recv_sem=br_sem.at[c],
                device_id={"band": to},
                device_id_type=MESH,
            ).start()
            return 0

        lax.fori_loop(1, N_BAND, one, 0)
        recv[c, band] = send[c, band]

    row = lax.broadcasted_iota(jnp.int32, (128, 128), 0)
    col = lax.broadcasted_iota(jnp.int32, (128, 128), 1)
    eye = (row == col).astype(jnp.bfloat16)

    def own_copy(c):
        return pltpu.make_async_remote_copy(
            src_ref=zsend.at[c, z // 2], dst_ref=zrecv.at[c, z],
            send_sem=zs_sem.at[c, 0], recv_sem=zr_sem.at[c, 0],
            device_id=partner_dev, device_id_type=MESH,
        )

    def direct_copy(c, d):
        at, dev = zdev({1: -sign, 2: 2 * sign, 3: -3 * sign}[d])
        return pltpu.make_async_remote_copy(
            src_ref=zsend.at[c, at // 2], dst_ref=zrecv.at[c, z],
            send_sem=zs_sem.at[c, d], recv_sem=zr_sem.at[c, d],
            device_id=dev, device_id_type=MESH,
        )

    def relay_copy(c, d):
        source, _ = zdev(-d * sign)
        return pltpu.make_async_remote_copy(
            src_ref=zrecv.at[c, source], dst_ref=zrecv.at[c, source],
            send_sem=rs_sem.at[c, d - 1], recv_sem=rr_sem.at[c, d - 1],
            device_id=partner_dev, device_id_type=MESH,
        )

    def turn(c):
        got = recv.at[c, pl.ds(0, N_BAND - 1)]
        pltpu.make_async_copy(got, got, br_sem.at[c]).wait()
        half = N_BAND // 2
        for part in range(2):
            rows = recv[c, part * half:(part + 1) * half].astype(jnp.float32).reshape(half * lat, 128)
            turned = lax.dot_general(
                eye, rows.astype(jnp.bfloat16), (((1,), (1,)), ((), ())),
                preferred_element_type=jnp.float32,
            ).astype(jnp.bfloat16)
            zsend[c, :, :, part * half * lat:(part + 1) * half * lat] = turned.reshape(4, 32, half * lat)
        own_copy(c).start()
        for d in (2, 3, 1):
            direct_copy(c, d).start()
        zrecv[c, z] = zsend[c, z // 2]

    def relay(c):
        for d in (1, 2, 3):
            direct_copy(c, d).wait_recv()
            relay_copy(c, d).start()

    def legendre(c):
        own_copy(c).wait_recv()
        for d in (1, 2, 3):
            relay_copy(c, d).wait_recv()
        load_leg(c).wait()

        def one(m, _):
            rows = pl.ds(pl.multiple_of(m * 16, 16), 16)
            data = zrecv[c, :, rows, :].reshape(128, zrecv.shape[3])
            out = jnp.dot(data, leg[2 * c + m], preferred_element_type=jnp.float32)
            out = out.reshape(4, 2, 2, 8, out.shape[1])
            for r in range(2):
                for f in range(4):
                    both = jnp.concatenate([out[f, 0, r], out[f, 1, r]], axis=0)
                    out_ref[2 * c + m, r, f] = both.astype(jnp.bfloat16)
            return 0

        lax.fori_loop(0, 2, one, 0)

    n_tiles = g.shape[1] // 128
    pairs = (n_tiles + 1) // 2
    pair_rows = 2 * lat

    def block_patch():
        def tile_rows(t):
            cols = pl.ds(pl.multiple_of(t * 128, 128), 128)
            return g[:, cols].astype(jnp.float32)

        def put(u, first, second):
            rows = pl.ds(pl.multiple_of(u * pair_rows, 16), pair_rows)
            for l in range(8):
                span = slice(l * lat, (l + 1) * lat)
                both = jnp.concatenate([first[span], second[span]], axis=0)
                patch[rows, l * 128:(l + 1) * 128] = both.astype(jnp.bfloat16)

        def one(u, _):
            put(u, tile_rows(2 * u), tile_rows(2 * u + 1))
            return 0

        lax.fori_loop(0, n_tiles // 2, one, 0)
        if n_tiles % 2:
            last = tile_rows(n_tiles - 1)
            put(n_tiles // 2, last, jnp.zeros_like(last))
        end = pairs * pair_rows
        patch[end:, :] = jnp.zeros((PATCH_ROWS - end, patch.shape[1]), jnp.bfloat16)
        small[0].wait()
        chosen = blocks[...].astype(jnp.float32)
        at_lat = jnp.floor((chosen + 0.5) * (1.0 / n_tiles))
        ids[...] = (chosen - at_lat * n_tiles) * lat + at_lat

    def column_copy(kind, to, from_buf, to_buf):
        return pltpu.make_async_remote_copy(
            src_ref=from_buf.at[to], dst_ref=to_buf.at[z],
            send_sem=col_sem.at[2 * kind], recv_sem=col_sem.at[2 * kind + 1],
            device_id={"sec": lax.rem(to, 2), "fld": to // 2}, device_id_type=MESH,
        )

    def column_wait(kind, is_recv, buf):
        part = buf.at[pl.ds(0, N_Z - 1)]
        pltpu.make_async_copy(part, part, col_sem.at[2 * kind + is_recv]).wait()

    def turn_patch():
        small[1].wait()

        def one(i, _):
            rows = pl.ds(pl.multiple_of(i * 128, 128), 128)
            for l in range(8):
                block = patch[rows, l * 128:(l + 1) * 128].astype(jnp.float32)
                patch_t[l * 128:(l + 1) * 128, rows] = jnp.transpose(block).astype(jnp.bfloat16)
            return 0

        lax.fori_loop(0, PATCH_ROWS // 128, one, 0)
        for place in range(N_Z):
            span = slice(place * 128, (place + 1) * 128)
            interp_t[:, span] = jnp.transpose(interp[span, :].astype(jnp.float32))

    def gather_state():
        row = lax.broadcasted_iota(jnp.int32, (PATCH_ROWS, 128), 0).astype(jnp.float32)

        def one(i, _):
            hot = jnp.concatenate(
                [(ids[pl.ds(2 * i + k, 1), :] == row).astype(jnp.bfloat16) for k in range(2)], axis=1
            )
            picked = jnp.dot(patch_t[...], hot, preferred_element_type=jnp.float32)
            factor = interp_t[:, pl.ds(pl.multiple_of(i * 256, 256), 256)]
            sums = [
                jnp.sum(picked[l * 128:(l + 1) * 128] * factor, axis=0, keepdims=True)
                for l in range(8)
            ]
            level = jnp.concatenate(sums, axis=0)
            for k in range(2):
                state_send[2 * i + k] = level[:, k * 128:(k + 1) * 128]
            return 0

        lax.fori_loop(0, N_Z // 2, one, 0)

        def send_state(k, _):
            column_copy(0, lax.rem(z + k, N_Z), state_send, state_recv).start()
            return 0

        lax.fori_loop(1, N_Z, send_state, 0)
        state_recv[z] = state_send[z]
        small[2].wait()
        small[3].wait()
        small[4].wait()
        inverse_wide[...] = inverse[...].astype(jnp.float32)

    def solve_columns():
        column_wait(0, 1, state_recv)
        state = state_recv[...].reshape(64, 128).astype(jnp.bfloat16)

        def sources(i, _):
            cols = pl.ds(pl.multiple_of(i * 256, 256), 256)
            gates = lax.dot_general(
                weights[:, cols], state, (((0,), (0,)), ((), ())), preferred_element_type=jnp.float32
            )
            source[cols, :] = jax.nn.softplus(gates)
            return 0

        lax.fori_loop(0, weights.shape[1] // 256, sources, 0)
        spec_bands = inverse.shape[1]
        flux_rows = inverse.shape[0] // 32

        sums = []
        for q in range(flux_rows):
            factor = inverse_wide[pl.ds(q, 32, stride=32), :].astype(jnp.bfloat16)
            value = source[pl.ds(q, spec_bands, stride=32), :].astype(jnp.bfloat16)
            sums.append(jnp.dot(factor, value, preferred_element_type=jnp.float32))
        while len(sums) > 1:
            sums = [first + second for first, second in zip(sums[::2], sums[1::2])]
        flux = sums[0]
        row16 = lax.broadcasted_iota(jnp.int32, (16, 128), 0)

        def drop(rows):
            above = jnp.where(row16 < 15, pltpu.roll(rows, 15, 0), 0.0)
            return rows - above

        heat = drop(flux[:16]) - drop(flux[16:])
        slot = (z * 128 + lax.broadcasted_iota(jnp.int32, (1, 128), 1)).astype(jnp.float32)
        at = lax.broadcasted_iota(jnp.int32, (1, N_BAND), 1)
        live = jnp.sum(
            jnp.where(at == band, counts[...].astype(jnp.float32), 0.0), axis=1, keepdims=True
        )
        heat = jnp.where(slot < live, heat, 0.0)
        heat = heat.astype(jnp.bfloat16).astype(jnp.float32)
        for group in range(N_Z):
            rows = heat[(group // 4) * 8:(group // 4) * 8 + 8]
            shift = (8 - 2 * (group % 4)) % 8
            heat_send[2 * (group % 4) + group // 4] = pltpu.roll(rows, shift, 0) if shift else rows

        def send_heat(k, _):
            column_copy(1, lax.rem(z + k, N_Z), heat_send, heat_recv).start()
            return 0

        lax.fori_loop(1, N_Z, send_heat, 0)

    def scatter_heat():
        heat_recv[z] = heat_send[z]
        column_wait(1, 1, heat_recv)
        step = lax.broadcasted_iota(jnp.int32, (pair_rows, 128), 0)

        def one(u, _):
            row = (step + u * pair_rows).astype(jnp.float32)
            parts = [[], []]
            for place in range(N_Z):
                hit = ids[place:place + 1, :] == row
                for l in range(2):
                    parts[l].append(
                        jnp.where(hit, heat_recv[place, l:l + 1, :], 0.0).astype(jnp.bfloat16)
                    )
            rows = jnp.concatenate([jnp.concatenate(p, axis=1) for p in parts], axis=0)
            summed = jnp.dot(rows, interp[...], preferred_element_type=jnp.float32)
            for l in range(2):
                for t in range(2):
                    value = summed[l * pair_rows + t * lat:l * pair_rows + (t + 1) * lat]
                    cols = pl.ds(pl.multiple_of((2 * u + t) * 128, 128), 128)

                    def put():
                        heat_ref[l, :, cols] = value.astype(jnp.bfloat16)

                    if t == 0:
                        put()
                    else:
                        pl.when(2 * u + 1 < n_tiles)(put)
            return 0

        lax.fori_loop(0, pairs, one, 0)

    dft(0)
    for load in small:
        load.start()
    for c in range(CHUNKS):
        load_leg(c).start()
    pl.semaphore_wait(barrier, N_BAND - 1 + N_Z - 1)
    send_bands(0)
    dft(1)
    send_bands(1)
    block_patch()
    turn_patch()
    gather_state()
    turn(0)
    dft(2)
    send_bands(2)
    turn(1)
    relay(0)
    turn(2)
    solve_columns()
    relay(1)
    legendre(0)
    relay(2)
    legendre(1)
    scatter_heat()
    legendre(2)

    column_wait(0, 0, state_send)
    column_wait(1, 0, heat_send)
    for c in range(CHUNKS):
        sent = send.at[c, pl.ds(0, N_BAND - 1)]
        pltpu.make_async_copy(sent, sent, bs_sem.at[c]).wait()
        own_copy(c).wait_send()
        for d in (1, 2, 3):
            direct_copy(c, d).wait_send()
            relay_copy(c, d).wait_send()


def body(grid, legendre, counts, blocks, interp, source_weights, inverses):
    lev_s, lat_d, lon = grid.shape[1:]
    wave_dev, lats, degrees = legendre.shape
    n_fld = lax.axis_size("fld")
    n_sec = lax.axis_size("sec")
    slots, width = interp.shape
    rows_in, sources = source_weights.shape
    spec_bands, flux_rows, _ = inverses.shape
    table = jnp.asarray(dft_table(lon, wave_dev, n_fld))
    flat = grid.reshape(lev_s * lat_d, lon)
    inv_rows = jnp.transpose(inverses, (1, 2, 0)).reshape(flux_rows * flux_rows, spec_bands)
    lev_out = n_sec * lev_s // (n_sec * n_fld)
    bf16, f32 = jnp.bfloat16, jnp.float32
    spectral, heating = pl.pallas_call(
        kernel,
        out_shape=(
            pltpu.VMEM((wave_dev, 2, n_fld, n_sec * lev_s, degrees), bf16),
            pltpu.VMEM((lev_out, lat_d, lon), bf16),
        ),
        in_specs=[pl.BlockSpec(memory_space=pltpu.HBM)] * 8,
        out_specs=(
            pl.BlockSpec(memory_space=pltpu.VMEM),
            pl.BlockSpec(memory_space=pltpu.VMEM),
        ),
        scratch_shapes=[
            pltpu.VMEM(flat.shape, bf16),
            pltpu.VMEM(table.shape, bf16),
            pltpu.VMEM(legendre.shape, bf16),
            pltpu.VMEM((CHUNKS, N_BAND, lat_d, 128), bf16),
            pltpu.VMEM((CHUNKS, N_BAND, lat_d, 128), bf16),
            pltpu.VMEM((CHUNKS, n_fld, 32, lats), bf16),
            pltpu.VMEM((CHUNKS, N_Z, 32, lats), bf16),
            pltpu.VMEM((1, N_BAND), jnp.int32),
            pltpu.VMEM((N_Z, 128), jnp.int32),
            pltpu.VMEM(interp.shape, bf16),
            pltpu.VMEM(source_weights.shape, bf16),
            pltpu.VMEM(inv_rows.shape, bf16),
            pltpu.VMEM((N_Z, 128), f32),
            pltpu.VMEM((PATCH_ROWS, lev_s * width), bf16),
            pltpu.VMEM((lev_s * width, PATCH_ROWS), bf16),
            pltpu.VMEM((width, slots), f32),
            pltpu.VMEM(inv_rows.shape, f32),
            pltpu.VMEM((sources, 128), f32),
            pltpu.VMEM((N_Z, 8, 128), f32),
            pltpu.VMEM((N_Z, 8, 128), f32),
            pltpu.VMEM((N_Z, 8, 128), f32),
            pltpu.VMEM((N_Z, 8, 128), f32),
            pltpu.SemaphoreType.DMA((10,)),
            pltpu.SemaphoreType.DMA((CHUNKS,)),
            pltpu.SemaphoreType.DMA((CHUNKS,)),
            pltpu.SemaphoreType.DMA((CHUNKS, 4)),
            pltpu.SemaphoreType.DMA((CHUNKS, 4)),
            pltpu.SemaphoreType.DMA((CHUNKS, 3)),
            pltpu.SemaphoreType.DMA((CHUNKS, 3)),
            pltpu.SemaphoreType.DMA((5,)),
            pltpu.SemaphoreType.DMA((4,)),
        ],
        compiler_params=pltpu.CompilerParams(
            collective_id=0, has_side_effects=True, vmem_limit_bytes=62 * 2**20
        ),
    )(
        flat, table, legendre, counts.reshape(1, N_BAND), blocks.reshape(N_Z, 128), interp,
        source_weights, inv_rows,
    )
    return (spectral, heating)


def solution(mesh):
    return jax.shard_map(
        body,
        mesh=mesh,
        in_specs=(
            P("fld", "sec", "band", None),
            P(("band", "fld"), None, "sec"),
            P(),
            P("band"),
            P("band", None),
            P(),
            P(),
        ),
        out_specs=(P(("band", "fld"), None, None, None, "sec"), P(("sec", "fld"), "band", None)),
        check_vma=False,
    )
```

```python
import functools
import math

import jax
import jax.numpy as jnp
import ml_dtypes
import numpy as np
from jax import lax
from jax.experimental import pallas as pl
from jax.experimental.pallas import tpu as pltpu
from jax.sharding import PartitionSpec as P

MESH = pl.DeviceIdType.MESH
N_BAND = 32
N_Z = 8
CHUNKS = 3
PATCH_ROWS = 896


def dft_table(lon, wave_dev, n_fld):
    waves = wave_dev * N_BAND * n_fld
    per_chunk = wave_dev // CHUNKS
    place = np.arange(lon, dtype=np.int64)
    wave = np.zeros((CHUNKS, 2, 2, n_fld, per_chunk, 2, 8), np.int64)
    part = np.zeros_like(wave)
    c, h, t, f, m, r, i = np.indices(wave.shape)
    band = (h * 2 + t) * 8 + i
    wave = (band * n_fld + f) * wave_dev + c * per_chunk + m
    part = r
    wave = wave.reshape(CHUNKS * 2, 256)
    part = part.reshape(CHUNKS * 2, 256)
    phase = (place[None, :, None] * wave[:, None, :]) % lon
    angle = phase.astype(np.float32) * np.float32(2.0 * math.pi / lon)
    values = np.where(part[:, None, :] == 0, np.cos(angle), -np.sin(angle))
    return (values.astype(np.float32) * np.float32(1.0 / math.sqrt(lon))).astype(ml_dtypes.bfloat16)


def transpose_levels(rows):
    lane = lax.broadcasted_iota(jnp.int32, rows[0].shape, 1)
    for bit in (1, 2, 4):
        high = (lane & bit) != 0
        out = list(rows)
        for l in range(8):
            if l & bit:
                continue
            a, b = rows[l], rows[l + bit]
            out[l] = jnp.where(high, pltpu.roll(b, bit, 1), a)
            out[l + bit] = jnp.where(high, b, pltpu.roll(a, 128 - bit, 1))
        rows = out
    return rows


def kernel(
    grid_hbm, tab_hbm, leg_hbm, counts_hbm, blocks_hbm, interp_hbm, weights_hbm, inverse_hbm,
    out_ref, heat_ref,
    g, tab, leg, send, recv, zsend, zrecv,
    counts, blocks, interp, weights, inverse,
    ids, patch, patch_t, interp_t, inverse_wide, source, state_send, state_recv, heat_send, heat_recv,
    load_sem, bs_sem, br_sem, zs_sem, zr_sem, rs_sem, rr_sem, small_sem, col_sem,
):
    lat = send.shape[2]
    band = lax.axis_index("band")
    z = lax.axis_index("fld") * 2 + lax.axis_index("sec")
    sign = 1 - 2 * lax.rem(z, 2)

    def zdev(step):
        at = lax.rem(z + step + 2 * N_Z, N_Z)
        return at, {"sec": lax.rem(at, 2), "fld": at // 2}

    partner, partner_dev = zdev(sign)

    def load_tab(t):
        return pltpu.make_async_copy(tab_hbm.at[t], tab.at[t], load_sem.at[t])

    def load_leg(c):
        return pltpu.make_async_copy(
            leg_hbm.at[pl.ds(2 * c, 2)], leg.at[pl.ds(2 * c, 2)], load_sem.at[7 + c]
        )

    load_g = pltpu.make_async_copy(grid_hbm, g, load_sem.at[6])
    load_g.start()
    load_tab(0).start()

    barrier = pltpu.get_barrier_semaphore()

    def greet(k, _):
        pl.semaphore_signal(
            barrier, inc=1, device_id={"band": lax.rem(band + k, N_BAND)}, device_id_type=MESH
        )
        return 0

    lax.fori_loop(1, N_BAND, greet, 0)
    for d in range(1, N_Z):
        pl.semaphore_signal(barrier, inc=1, device_id=zdev(d)[1], device_id_type=MESH)
    load_tab(1).start()
    small = [
        pltpu.make_async_copy(source_ref, target_ref, small_sem.at[i])
        for i, (source_ref, target_ref) in enumerate(
            ((blocks_hbm, blocks), (interp_hbm, interp), (weights_hbm, weights),
             (inverse_hbm, inverse), (counts_hbm, counts))
        )
    ]
    load_g.wait()

    def dft_step(t, _):
        c = t // 2
        load_tab(t).wait()

        @pl.when(t < 2 * CHUNKS - 2)
        def _():
            load_tab(t + 2).start()

        coeffs = jnp.dot(g[...], tab[t], preferred_element_type=jnp.float32)
        for tile in range(2):
            rows = [coeffs[l * lat:(l + 1) * lat, tile * 128:(tile + 1) * 128] for l in range(8)]
            rows = transpose_levels(rows)
            for i in range(8):
                send[c, lax.rem(t, 2) * 16 + tile * 8 + i] = rows[i].astype(jnp.bfloat16)
        return 0

    def dft(c):
        lax.fori_loop(2 * c, 2 * c + 2, dft_step, 0)

    def send_bands(c):
        def one(k, _):
            to = lax.rem(band + k, N_BAND)
            pltpu.make_async_remote_copy(
                src_ref=send.at[c, to],
                dst_ref=recv.at[c, band],
                send_sem=bs_sem.at[c],
                recv_sem=br_sem.at[c],
                device_id={"band": to},
                device_id_type=MESH,
            ).start()
            return 0

        lax.fori_loop(1, N_BAND, one, 0)
        recv[c, band] = send[c, band]

    row = lax.broadcasted_iota(jnp.int32, (128, 128), 0)
    col = lax.broadcasted_iota(jnp.int32, (128, 128), 1)
    eye = (row == col).astype(jnp.bfloat16)

    def own_copy(c):
        return pltpu.make_async_remote_copy(
            src_ref=zsend.at[c, z // 2], dst_ref=zrecv.at[c, z],
            send_sem=zs_sem.at[c, 0], recv_sem=zr_sem.at[c, 0],
            device_id=partner_dev, device_id_type=MESH,
        )

    def direct_copy(c, d):
        at, dev = zdev({1: -sign, 2: 2 * sign, 3: -3 * sign}[d])
        return pltpu.make_async_remote_copy(
            src_ref=zsend.at[c, at // 2], dst_ref=zrecv.at[c, z],
            send_sem=zs_sem.at[c, d], recv_sem=zr_sem.at[c, d],
            device_id=dev, device_id_type=MESH,
        )

    def relay_copy(c, d):
        source, _ = zdev(-d * sign)
        return pltpu.make_async_remote_copy(
            src_ref=zrecv.at[c, source], dst_ref=zrecv.at[c, source],
            send_sem=rs_sem.at[c, d - 1], recv_sem=rr_sem.at[c, d - 1],
            device_id=partner_dev, device_id_type=MESH,
        )

    def turn(c):
        got = recv.at[c, pl.ds(0, N_BAND - 1)]
        pltpu.make_async_copy(got, got, br_sem.at[c]).wait()
        half = N_BAND // 2
        for part in range(2):
            rows = recv[c, part * half:(part + 1) * half].astype(jnp.float32).reshape(half * lat, 128)
            turned = lax.dot_general(
                eye, rows.astype(jnp.bfloat16), (((1,), (1,)), ((), ())),
                preferred_element_type=jnp.float32,
            ).astype(jnp.bfloat16)
            zsend[c, :, :, part * half * lat:(part + 1) * half * lat] = turned.reshape(4, 32, half * lat)
        own_copy(c).start()
        for d in (2, 3, 1):
            direct_copy(c, d).start()
        zrecv[c, z] = zsend[c, z // 2]

    def relay(c):
        for d in (1, 2, 3):
            direct_copy(c, d).wait_recv()
            relay_copy(c, d).start()

    def legendre(c):
        own_copy(c).wait_recv()
        for d in (1, 2, 3):
            relay_copy(c, d).wait_recv()
        load_leg(c).wait()

        def one(m, _):
            rows = pl.ds(pl.multiple_of(m * 16, 16), 16)
            data = zrecv[c, :, rows, :].reshape(128, zrecv.shape[3])
            out = jnp.dot(data, leg[2 * c + m], preferred_element_type=jnp.float32)
            out = out.reshape(4, 2, 2, 8, out.shape[1])
            for r in range(2):
                for f in range(4):
                    both = jnp.concatenate([out[f, 0, r], out[f, 1, r]], axis=0)
                    out_ref[2 * c + m, r, f] = both.astype(jnp.bfloat16)
            return 0

        lax.fori_loop(0, 2, one, 0)

    n_tiles = g.shape[1] // 128
    pairs = (n_tiles + 1) // 2
    pair_rows = 2 * lat

    def block_patch():
        def tile_rows(t):
            cols = pl.ds(pl.multiple_of(t * 128, 128), 128)
            return g[:, cols].astype(jnp.float32)

        def put(u, first, second):
            rows = pl.ds(pl.multiple_of(u * pair_rows, 16), pair_rows)
            for l in range(8):
                span = slice(l * lat, (l + 1) * lat)
                both = jnp.concatenate([first[span], second[span]], axis=0)
                patch[rows, l * 128:(l + 1) * 128] = both.astype(jnp.bfloat16)

        def one(u, _):
            put(u, tile_rows(2 * u), tile_rows(2 * u + 1))
            return 0

        lax.fori_loop(0, n_tiles // 2, one, 0)
        if n_tiles % 2:
            last = tile_rows(n_tiles - 1)
            put(n_tiles // 2, last, jnp.zeros_like(last))
        end = pairs * pair_rows
        patch[end:, :] = jnp.zeros((PATCH_ROWS - end, patch.shape[1]), jnp.bfloat16)
        small[0].wait()
        chosen = blocks[...].astype(jnp.float32)
        at_lat = jnp.floor((chosen + 0.5) * (1.0 / n_tiles))
        ids[...] = (chosen - at_lat * n_tiles) * lat + at_lat

    def column_copy(kind, to, from_buf, to_buf):
        return pltpu.make_async_remote_copy(
            src_ref=from_buf.at[to], dst_ref=to_buf.at[z],
            send_sem=col_sem.at[2 * kind], recv_sem=col_sem.at[2 * kind + 1],
            device_id={"sec": lax.rem(to, 2), "fld": to // 2}, device_id_type=MESH,
        )

    def column_wait(kind, is_recv, buf):
        part = buf.at[pl.ds(0, N_Z - 1)]
        pltpu.make_async_copy(part, part, col_sem.at[2 * kind + is_recv]).wait()

    def turn_patch():
        small[1].wait()

        def one(i, _):
            rows = pl.ds(pl.multiple_of(i * 128, 128), 128)
            for l in range(8):
                block = patch[rows, l * 128:(l + 1) * 128].astype(jnp.float32)
                patch_t[l * 128:(l + 1) * 128, rows] = jnp.transpose(block).astype(jnp.bfloat16)
            return 0

        lax.fori_loop(0, PATCH_ROWS // 128, one, 0)
        for place in range(N_Z):
            span = slice(place * 128, (place + 1) * 128)
            interp_t[:, span] = jnp.transpose(interp[span, :].astype(jnp.float32))

    def gather_state():
        row = lax.broadcasted_iota(jnp.int32, (PATCH_ROWS, 128), 0).astype(jnp.float32)

        def one(i, _):
            hot = jnp.concatenate(
                [(ids[pl.ds(2 * i + k, 1), :] == row).astype(jnp.bfloat16) for k in range(2)], axis=1
            )
            picked = jnp.dot(patch_t[...], hot, preferred_element_type=jnp.float32)
            factor = interp_t[:, pl.ds(pl.multiple_of(i * 256, 256), 256)]
            sums = [
                jnp.sum(picked[l * 128:(l + 1) * 128] * factor, axis=0, keepdims=True)
                for l in range(8)
            ]
            level = jnp.concatenate(sums, axis=0)
            for k in range(2):
                state_send[2 * i + k] = level[:, k * 128:(k + 1) * 128]
            return 0

        lax.fori_loop(0, N_Z // 2, one, 0)

        def send_state(k, _):
            column_copy(0, lax.rem(z + k, N_Z), state_send, state_recv).start()
            return 0

        lax.fori_loop(1, N_Z, send_state, 0)
        state_recv[z] = state_send[z]
        small[2].wait()
        small[3].wait()
        small[4].wait()
        inverse_wide[...] = inverse[...].astype(jnp.float32)

    def solve_columns():
        column_wait(0, 1, state_recv)
        state = state_recv[...].reshape(64, 128).astype(jnp.bfloat16)

        def sources(i, _):
            cols = pl.ds(pl.multiple_of(i * 256, 256), 256)
            gates = lax.dot_general(
                weights[:, cols], state, (((0,), (0,)), ((), ())), preferred_element_type=jnp.float32
            )
            source[cols, :] = jax.nn.softplus(gates)
            return 0

        lax.fori_loop(0, weights.shape[1] // 256, sources, 0)
        spec_bands = inverse.shape[1]
        flux_rows = inverse.shape[0] // 32

        sums = []
        for q in range(flux_rows):
            factor = inverse_wide[pl.ds(q, 32, stride=32), :].astype(jnp.bfloat16)
            value = source[pl.ds(q, spec_bands, stride=32), :].astype(jnp.bfloat16)
            sums.append(jnp.dot(factor, value, preferred_element_type=jnp.float32))
        while len(sums) > 1:
            sums = [first + second for first, second in zip(sums[::2], sums[1::2])]
        flux = sums[0]
        row16 = lax.broadcasted_iota(jnp.int32, (16, 128), 0)

        def drop(rows):
            above = jnp.where(row16 < 15, pltpu.roll(rows, 15, 0), 0.0)
            return rows - above

        heat = drop(flux[:16]) - drop(flux[16:])
        slot = (z * 128 + lax.broadcasted_iota(jnp.int32, (1, 128), 1)).astype(jnp.float32)
        at = lax.broadcasted_iota(jnp.int32, (1, N_BAND), 1)
        live = jnp.sum(
            jnp.where(at == band, counts[...].astype(jnp.float32), 0.0), axis=1, keepdims=True
        )
        heat = jnp.where(slot < live, heat, 0.0)
        heat = heat.astype(jnp.bfloat16).astype(jnp.float32)
        for group in range(N_Z):
            rows = heat[(group // 4) * 8:(group // 4) * 8 + 8]
            shift = (8 - 2 * (group % 4)) % 8
            heat_send[2 * (group % 4) + group // 4] = pltpu.roll(rows, shift, 0) if shift else rows

        def send_heat(k, _):
            column_copy(1, lax.rem(z + k, N_Z), heat_send, heat_recv).start()
            return 0

        lax.fori_loop(1, N_Z, send_heat, 0)

    def scatter_heat():
        heat_recv[z] = heat_send[z]
        column_wait(1, 1, heat_recv)
        step = lax.broadcasted_iota(jnp.int32, (pair_rows, 128), 0)

        def one(u, _):
            row = (step + u * pair_rows).astype(jnp.float32)
            parts = [[], []]
            for place in range(N_Z):
                hit = ids[place:place + 1, :] == row
                for l in range(2):
                    parts[l].append(
                        jnp.where(hit, heat_recv[place, l:l + 1, :], 0.0).astype(jnp.bfloat16)
                    )
            rows = jnp.concatenate([jnp.concatenate(p, axis=1) for p in parts], axis=0)
            summed = jnp.dot(rows, interp[...], preferred_element_type=jnp.float32)
            for l in range(2):
                for t in range(2):
                    value = summed[l * pair_rows + t * lat:l * pair_rows + (t + 1) * lat]
                    cols = pl.ds(pl.multiple_of((2 * u + t) * 128, 128), 128)

                    def put():
                        heat_ref[l, :, cols] = value.astype(jnp.bfloat16)

                    if t == 0:
                        put()
                    else:
                        pl.when(2 * u + 1 < n_tiles)(put)
            return 0

        lax.fori_loop(0, pairs, one, 0)

    dft(0)
    for load in small:
        load.start()
    for c in range(CHUNKS):
        load_leg(c).start()
    pl.semaphore_wait(barrier, N_BAND - 1 + N_Z - 1)
    send_bands(0)
    dft(1)
    send_bands(1)
    block_patch()
    turn_patch()
    gather_state()
    turn(0)
    dft(2)
    send_bands(2)
    turn(1)
    relay(0)
    turn(2)
    solve_columns()
    relay(1)
    legendre(0)
    relay(2)
    legendre(1)
    scatter_heat()
    legendre(2)

    column_wait(0, 0, state_send)
    column_wait(1, 0, heat_send)
    for c in range(CHUNKS):
        sent = send.at[c, pl.ds(0, N_BAND - 1)]
        pltpu.make_async_copy(sent, sent, bs_sem.at[c]).wait()
        own_copy(c).wait_send()
        for d in (1, 2, 3):
            direct_copy(c, d).wait_send()
            relay_copy(c, d).wait_send()


def body(grid, legendre, counts, blocks, interp, source_weights, inverses):
    lev_s, lat_d, lon = grid.shape[1:]
    wave_dev, lats, degrees = legendre.shape
    n_fld = lax.axis_size("fld")
    n_sec = lax.axis_size("sec")
    slots, width = interp.shape
    rows_in, sources = source_weights.shape
    spec_bands, flux_rows, _ = inverses.shape
    table = jnp.asarray(dft_table(lon, wave_dev, n_fld))
    flat = grid.reshape(lev_s * lat_d, lon)
    inv_rows = jnp.transpose(inverses, (1, 2, 0)).reshape(flux_rows * flux_rows, spec_bands)
    lev_out = n_sec * lev_s // (n_sec * n_fld)
    bf16, f32 = jnp.bfloat16, jnp.float32
    spectral, heating = pl.pallas_call(
        kernel,
        out_shape=(
            pltpu.VMEM((wave_dev, 2, n_fld, n_sec * lev_s, degrees), bf16),
            pltpu.VMEM((lev_out, lat_d, lon), bf16),
        ),
        in_specs=[pl.BlockSpec(memory_space=pltpu.HBM)] * 8,
        out_specs=(
            pl.BlockSpec(memory_space=pltpu.VMEM),
            pl.BlockSpec(memory_space=pltpu.VMEM),
        ),
        scratch_shapes=[
            pltpu.VMEM(flat.shape, bf16),
            pltpu.VMEM(table.shape, bf16),
            pltpu.VMEM(legendre.shape, bf16),
            pltpu.VMEM((CHUNKS, N_BAND, lat_d, 128), bf16),
            pltpu.VMEM((CHUNKS, N_BAND, lat_d, 128), bf16),
            pltpu.VMEM((CHUNKS, n_fld, 32, lats), bf16),
            pltpu.VMEM((CHUNKS, N_Z, 32, lats), bf16),
            pltpu.VMEM((1, N_BAND), jnp.int32),
            pltpu.VMEM((N_Z, 128), jnp.int32),
            pltpu.VMEM(interp.shape, bf16),
            pltpu.VMEM(source_weights.shape, bf16),
            pltpu.VMEM(inv_rows.shape, bf16),
            pltpu.VMEM((N_Z, 128), f32),
            pltpu.VMEM((PATCH_ROWS, lev_s * width), bf16),
            pltpu.VMEM((lev_s * width, PATCH_ROWS), bf16),
            pltpu.VMEM((width, slots), f32),
            pltpu.VMEM(inv_rows.shape, f32),
            pltpu.VMEM((sources, 128), f32),
            pltpu.VMEM((N_Z, 8, 128), f32),
            pltpu.VMEM((N_Z, 8, 128), f32),
            pltpu.VMEM((N_Z, 8, 128), f32),
            pltpu.VMEM((N_Z, 8, 128), f32),
            pltpu.SemaphoreType.DMA((10,)),
            pltpu.SemaphoreType.DMA((CHUNKS,)),
            pltpu.SemaphoreType.DMA((CHUNKS,)),
            pltpu.SemaphoreType.DMA((CHUNKS, 4)),
            pltpu.SemaphoreType.DMA((CHUNKS, 4)),
            pltpu.SemaphoreType.DMA((CHUNKS, 3)),
            pltpu.SemaphoreType.DMA((CHUNKS, 3)),
            pltpu.SemaphoreType.DMA((5,)),
            pltpu.SemaphoreType.DMA((4,)),
        ],
        compiler_params=pltpu.CompilerParams(
            collective_id=0, has_side_effects=True, vmem_limit_bytes=62 * 2**20
        ),
    )(
        flat, table, legendre, counts.reshape(1, N_BAND), blocks.reshape(N_Z, 128), interp,
        source_weights, inv_rows,
    )
    return (spectral, heating)


def solution(mesh):
    return jax.shard_map(
        body,
        mesh=mesh,
        in_specs=(
            P("fld", "sec", "band", None),
            P(("band", "fld"), None, "sec"),
            P(),
            P("band"),
            P("band", None),
            P(),
            P(),
        ),
        out_specs=(P(("band", "fld"), None, None, None, "sec"), P(("sec", "fld"), "band", None)),
        check_vma=False,
    )
```
